32 devices in a mesh: lat: 4 (over y, x), lev: 8 (over z, core).
Axes of the slice: x: 2, y: 2, z: 4, core: 2. Of those that a mesh axis runs over, the one named last changes fastest.
Arguments:
- grid_gradient: float32 [64, 640, 1280], P('lev', 'lat'), may hold values from -0.4375 to 0.4375
- legendre: bfloat16 [640, 640, 320], P('lat', 'lev'), may hold values from -0.15625 to 0.15625
- assign: int32 [640], replicated, may hold values from 0 to 639, as said below
Outputs:
- coeff_gradient: bfloat16 [640, 640, 128], P('lat', 'lev')
The draws below stay inside these ranges and needn't reach their ends.
Inputs may be any that keep to these rules, and one draw needn't show every extreme that they name: `assign`: each wavenumber appears once; slots 2q and 2q + 1 hold two wavenumbers that sum to 639.
All inputs are finite; a program needn't handle non-finite values.
Results may differ from the reference program's by a relative error of at most 0.0059.
Values may be sent and summed in bfloat16 or wider, within the bound.
No kernel may reach another device: no remote copies, remote signals or barrier semaphores. Data moves between devices by JAX's collectives and lax.ppermute only.
A program may use at most 128 MiB of HBM per device.

```python
import jax
import jax.numpy as jnp
from jax import lax

M = 640
NLAT = 640
NLON = 1280
NH = 320
FL = 64


def draw_assign(key, part):
    pairs = jax.random.permutation(jax.random.fold_in(key, 11), M // 2).astype(jnp.int32)
    flips = jax.random.randint(jax.random.fold_in(key, 12), (M // 2,), 0, 2).astype(jnp.int32)
    upper = (M - 1 - pairs).astype(jnp.int32)
    first = jnp.where(flips == 1, upper, pairs)
    second = jnp.where(flips == 1, pairs, upper)
    return jnp.stack([first, second], axis=1).reshape(M).astype(jnp.int32)


def levels(key, extent, shards, low, high):
    gain, own = 1.0, jax.random.fold_in(key, 6)
    for position, parts in shards:
        draws = jnp.exp(jax.random.uniform(jax.random.fold_in(own, position), (parts,), jnp.float32, low / len(shards), high / len(shards)))
        gain = gain * jnp.repeat(draws, extent[position] // parts).reshape([-1 if axis == position else 1 for axis in range(len(extent))])
    return gain


def normal_values(own_key, extent, width, limit, cuts=(), held_as=jnp.bfloat16):
    factor_of = levels(own_key, extent, cuts, -0.22, 0.18) if cuts else 1.0
    values = jax.random.normal(own_key, extent, jnp.float32) * width * factor_of
    return jnp.minimum(jnp.maximum(values, -limit), limit).astype(held_as)


def setup_inputs(seed: int = 0) -> dict:
    keys = jax.random.split(jax.random.key(seed), 4)
    grid_gradient = normal_values(keys[0], (FL, NLAT, NLON), 0.03, 0.4375, ((0, 8), (1, 4)), jnp.float32)
    legendre = normal_values(keys[1], (M, M, NH), (2 * M) ** -0.5, 0.15625, ((0, 4), (1, 8)))
    assign = draw_assign(jax.random.fold_in(keys[3], 71), 0)
    return dict(grid_gradient=grid_gradient, legendre=legendre, assign=assign)


def reference(grid_gradient, legendre, assign):
    transform = jnp.fft.rfft(grid_gradient, axis=-1)[..., :M]
    modes = jnp.arange(M)
    weight = jnp.where(modes == 0, 1.0, 2.0).astype(jnp.float32)
    real_part = jnp.real(transform).astype(jnp.float32) * weight
    imag_part = jnp.imag(transform).astype(jnp.float32) * weight
    spec = jnp.stack([real_part, imag_part], axis=1).astype(jnp.bfloat16)
    north = spec[:, :, :NH, :].astype(jnp.float32)
    south = spec[:, :, ::-1, :][:, :, :NH, :].astype(jnp.float32)
    even = (north + south).astype(jnp.bfloat16)
    odd = (north - south).astype(jnp.bfloat16)
    degrees = jnp.arange(M)

    def one_slot(index):
        wave = assign[index]
        even_col = jnp.take(even, wave, axis=3)
        odd_col = jnp.take(odd, wave, axis=3)
        even_mat = jnp.transpose(even_col, (1, 0, 2)).reshape(2 * FL, NH)
        odd_mat = jnp.transpose(odd_col, (1, 0, 2)).reshape(2 * FL, NH)
        table = legendre[index]
        from_even = jnp.dot(table, even_mat.T, preferred_element_type=jnp.float32)
        from_odd = jnp.dot(table, odd_mat.T, preferred_element_type=jnp.float32)
        chosen = jnp.where((degrees % 2 == 0)[:, None], from_even, from_odd)
        valid = degrees < (M - wave)
        return jnp.where(valid[:, None], chosen, 0.0).astype(jnp.bfloat16)

    return lax.map(one_slot, jnp.arange(M).astype(jnp.int32))
```

```python
import functools
import math

import jax
import jax.numpy as jnp
from jax import lax
from jax.experimental import pallas as pl
from jax.experimental.pallas import tpu as pltpu
from jax.sharding import PartitionSpec as P

LANES = 128
VMEM_LIMIT = 48 * 1024 * 1024


def dot_nt(a, b):
    return lax.dot_general(a, b, (((1,), (1,)), ((), ())), preferred_element_type=jnp.float32)


def params():
    return pltpu.CompilerParams(vmem_limit_bytes=VMEM_LIMIT)


def hi_lo(x):
    hi = x.astype(jnp.bfloat16)
    return hi, (x - hi.astype(jnp.float32)).astype(jnp.bfloat16)


def fold_kernel(order_ref, grid_ref, out_ref):
    half = out_ref.shape[2]
    near, far = grid_ref[0, :, :half], grid_ref[0, :, half:]
    for parity, folded in enumerate((near + far, near - far)):
        for part, term in enumerate(hi_lo(folded)):
            moved = jnp.dot(order_ref[...], term, preferred_element_type=jnp.float32)
            out_ref[2 * parity + part] = moved.astype(jnp.bfloat16)


def fold_grid(grid, order):
    fields, rows, nlon = grid.shape
    half = nlon // 2
    return pl.pallas_call(
        fold_kernel,
        grid=(fields,),
        in_specs=[
            pl.BlockSpec((rows, rows), lambda f: (0, 0)),
            pl.BlockSpec((1, rows, nlon), lambda f: (f, 0, 0)),
        ],
        out_specs=pl.BlockSpec((4, None, rows, half), lambda f: (0, f, 0, 0)),
        out_shape=jax.ShapeDtypeStruct((4, fields, rows, half), jnp.bfloat16),
        compiler_params=params(),
        cost_estimate=pl.CostEstimate(
            flops=8 * fields * rows * rows * half, bytes_accessed=8 * fields * rows * nlon, transcendentals=0
        ),
        name="fold",
    )(order, grid)


def zonal_kernel(start, base_ref, step_ref, first_ref, grid_ref, out_ref, table_ref):
    groups, _, _, pairs, _ = out_ref.shape
    count = groups * pairs
    steps = step_ref.shape[3]

    @pl.when(pl.program_id(0) == 0)
    def _():
        for parity in range(2):
            cos0 = base_ref[parity, 0, start : start + count]
            sin0 = base_ref[parity, 1, start : start + count]
            for b in range(steps):
                cos1 = step_ref[parity, 0, start : start + count, b : b + 1]
                sin1 = step_ref[parity, 1, start : start + count, b : b + 1]
                both = (cos0 * cos1 - sin0 * sin1, -(sin0 * cos1 + cos0 * sin1))
                for c, table in enumerate(both):
                    for part, term in enumerate(hi_lo(table)):
                        table_ref[parity, part, c * count : (c + 1) * count, b * LANES : (b + 1) * LANES] = term

    found = []
    for parity in range(2):
        hi, lo = table_ref[parity, 0], table_ref[parity, 1]
        found.append(
            dot_nt(hi, grid_ref[2 * parity])
            + (dot_nt(lo, grid_ref[2 * parity]) + dot_nt(hi, grid_ref[2 * parity + 1]))
        )
    first = first_ref[start : start + count] > 0.5
    for c in range(2):
        even, odd = found[0][c * count : (c + 1) * count], found[1][c * count : (c + 1) * count]
        low = jnp.where(first, even, odd).astype(jnp.bfloat16)
        high = jnp.where(first, odd, even).astype(jnp.bfloat16)
        for g in range(groups):
            out_ref[g, 0, c] = low[g * pairs : (g + 1) * pairs]
            out_ref[g, 1, c] = high[g * pairs : (g + 1) * pairs]


def zonal(base, step, first, folded, groups, start, pairs):
    columns, half = folded.shape[1:]
    block = columns // 5 if columns % (5 * LANES) == 0 else columns
    count = groups * pairs
    return pl.pallas_call(
        functools.partial(zonal_kernel, start),
        grid=(columns // block,),
        in_specs=[
            pl.BlockSpec(base.shape, lambda n: (0, 0, 0, 0)),
            pl.BlockSpec(step.shape, lambda n: (0, 0, 0, 0)),
            pl.BlockSpec(first.shape, lambda n: (0, 0)),
            pl.BlockSpec((4, block, half), lambda n: (0, n, 0)),
        ],
        out_specs=pl.BlockSpec((groups, 2, 2, pairs, block), lambda n: (0, 0, 0, 0, n)),
        out_shape=jax.ShapeDtypeStruct((groups, 2, 2, pairs, columns), jnp.bfloat16),
        scratch_shapes=[pltpu.VMEM((2, 2, 2 * count, half), jnp.bfloat16)],
        compiler_params=params(),
        cost_estimate=pl.CostEstimate(
            flops=24 * count * columns * half, bytes_accessed=8 * columns * half, transcendentals=0
        ),
        name="zonal",
    )(base, step, first, folded)


def halves_kernel(fields, wide, in_ref, low_ref, high_ref, work_ref):
    groups, _, _, pairs, columns = in_ref.shape
    rows = columns // fields
    for which, out_ref in enumerate((low_ref, high_ref)):
        for c in range(2):
            parts = [in_ref[g, which, c].astype(jnp.float32) for g in range(groups)]
            sums = [parts[g] + parts[groups - 1 - g] for g in range(groups // 2)]
            gaps = [parts[g] - parts[groups - 1 - g] for g in range(groups // 2)]
            for f in range(fields):
                at = slice(f * rows, (f + 1) * rows)
                even = jnp.concatenate([x[:, at] for x in sums], axis=1)
                odd = jnp.concatenate([x[:, at] for x in gaps], axis=1)
                whole = jnp.concatenate([even[:, :wide], odd[:, :wide], even[:, wide:], odd[:, wide:]], axis=1)
                work_ref[:, c * fields + f, :] = whole
        out_ref[...] = work_ref[...].astype(jnp.bfloat16)


def halves(arrived, fields, wide):
    groups, _, _, pairs, columns = arrived.shape
    length = groups * columns // fields
    shape = jax.ShapeDtypeStruct((pairs, 2 * fields, length), jnp.bfloat16)
    return pl.pallas_call(
        functools.partial(halves_kernel, fields, wide),
        out_shape=(shape, shape),
        in_specs=[pl.BlockSpec(memory_space=pltpu.VMEM)],
        out_specs=(pl.BlockSpec(memory_space=pltpu.VMEM),) * 2,
        scratch_shapes=[pltpu.VMEM((pairs, 2 * fields, length), jnp.float32)],
        compiler_params=params(),
        cost_estimate=pl.CostEstimate(
            flops=pairs * 4 * fields * length, bytes_accessed=16 * pairs * fields * length, transcendentals=0
        ),
        name="halves",
    )(arrived)


def contract(table, mine, other, index, wide, order):
    chips, _, lines, length = mine.shape
    spec = jnp.concatenate(
        [ref[d, index] for d in range(chips) for ref in (mine, other)], axis=0
    )
    half = length // 2
    count = spec.shape[0]
    degrees = table.shape[0]
    even_row = lax.rem(lax.broadcasted_iota(jnp.int32, (degrees, 1), 0), 2) == 0
    main = dot_nt(table[:, :wide], jnp.concatenate([spec[:, :wide], spec[:, wide : 2 * wide]], axis=0))
    total = jnp.where(even_row, main[:, :count], main[:, count:])
    if half > wide:
        rest = table[:, wide:].astype(jnp.float32)
        rest = jnp.concatenate([jnp.where(even_row, rest, 0.0), jnp.where(even_row, 0.0, rest)], axis=1)
        total = total + dot_nt(rest.astype(jnp.bfloat16), spec[:, 2 * wide :])
    return jnp.dot(total.astype(jnp.bfloat16), order, preferred_element_type=jnp.float32)


def keep_valid(values, first_degree, wave, modes):
    degrees = first_degree + lax.broadcasted_iota(jnp.int32, (values.shape[0], 1), 0)
    return jnp.where(degrees < modes - wave, values, 0.0).astype(jnp.bfloat16)


def column_order(lev_id, chips, lines):
    fields = lines // 2
    count = 2 * chips * lines
    row = lax.broadcasted_iota(jnp.int32, (count, count), 0)
    column = lax.broadcasted_iota(jnp.int32, (count, count), 1)
    chip = lax.rem(row // (2 * lines) + lev_id // 2, chips)
    core = lax.rem(row // lines + lev_id, 2)
    c = lax.rem(row // fields, 2)
    target = c * (count // 2) + (2 * chip + core) * fields + lax.rem(row, fields)
    return jnp.where(column == target, 1.0, 0.0).astype(jnp.bfloat16)


def high_kernel(start, modes, wide, info_ref, waves_ref, order_ref, table_ref, given_ref, mine_ref, other_ref, own_ref, back_ref):
    pairs, degrees, _ = own_ref.shape
    block = pl.program_id(0)
    lev = info_ref[0]
    order = order_ref[...]

    def body(i, _):
        q = start + block * pairs + i
        swapped = waves_ref[2 * q] > waves_ref[2 * q + 1]
        slot = 2 * i + jnp.where(swapped, 0, 1)
        wave = jnp.maximum(waves_ref[2 * q], waves_ref[2 * q + 1])
        both = jnp.concatenate([table_ref[slot], given_ref[i]], axis=0)
        values = contract(both, mine_ref, other_ref, i, wide, order)
        own_ref[i] = keep_valid(values[:degrees], lev * degrees, wave, modes)
        back_ref[i] = keep_valid(values[degrees:], (lev - 2) * degrees, wave, modes)
        return 0

    lax.fori_loop(0, pairs, body, 0, unroll=2 if pairs % 2 == 0 else 1)


def low_kernel(start, modes, wide, info_ref, waves_ref, order_ref, table_ref, mine_ref, other_ref, own_ref, back_ref, *out_refs):
    out_ref = out_refs[-1]
    pairs, degrees, _ = own_ref.shape
    block = pl.program_id(0)
    lev = info_ref[0]
    order = order_ref[...]
    lowest = lev < 2

    def body(i, _):
        q = start + block * pairs + i
        swapped = waves_ref[2 * q] > waves_ref[2 * q + 1]
        slot = 2 * i + jnp.where(swapped, 1, 0)
        wave = jnp.minimum(waves_ref[2 * q], waves_ref[2 * q + 1])
        values = contract(table_ref[slot], mine_ref, other_ref, i, wide, order)
        out_ref[slot] = keep_valid(values, lev * degrees, wave, modes)
        out_ref[2 * i + jnp.where(swapped, 0, 1)] = jnp.where(lowest, back_ref[i], own_ref[i])
        return 0

    lax.fori_loop(0, pairs, body, 0, unroll=2 if pairs % 2 == 0 else 1)


def legendre_specs(start, block, degrees, half, mine, count):
    chips, _, lines, length = mine.shape
    smem = pl.BlockSpec(memory_space=pltpu.SMEM)
    offset = start // block
    piece = pl.BlockSpec((chips, block, lines, length), lambda i: (0, i, 0, 0))
    return [smem, smem, pl.BlockSpec((count, count), lambda i: (0, 0)),
            pl.BlockSpec((2 * block, degrees, half), lambda i: (offset + i, 0, 0))], piece


def block_pairs(start, pairs):
    for size in (8, 4, 2):
        if start % size == 0 and pairs % size == 0:
            return size
    return pairs if start % pairs == 0 else 1


def high_slots(start, modes, wide, info, waves, order, table, given, mine, other):
    pairs, degrees, half = given.shape
    count = order.shape[0]
    block = block_pairs(start, pairs)
    shared, piece = legendre_specs(start, block, degrees, half, mine, count)
    result = pl.BlockSpec((block, degrees, count), lambda i: (i, 0, 0))
    shape = jax.ShapeDtypeStruct((pairs, degrees, count), jnp.bfloat16)
    return pl.pallas_call(
        functools.partial(high_kernel, start, modes, wide),
        grid=(pairs // block,),
        in_specs=shared + [pl.BlockSpec((block, degrees, half), lambda i: (i, 0, 0)), piece, piece],
        out_specs=(result, result),
        out_shape=(shape, shape),
        compiler_params=params(),
        cost_estimate=pl.CostEstimate(
            flops=8 * pairs * degrees * half * count, bytes_accessed=pairs * count * half * 8, transcendentals=0
        ),
        name="high_slots",
    )(info, waves, order, table, given, mine, other)


def low_slots(start, modes, wide, info, waves, order, table, mine, other, own, back, out):
    pairs, degrees, count = own.shape
    slots, _, half = table.shape
    block = block_pairs(start, pairs)
    offset = start // block
    shared, piece = legendre_specs(start, block, degrees, half, mine, count)
    given = pl.BlockSpec((block, degrees, count), lambda i: (i, 0, 0))
    operands = [info, waves, order, table, mine, other, own, back]
    in_specs = shared + [piece, piece, given, given]
    aliases = {}
    if out is not None:
        aliases = {len(operands): 0}
        operands.append(out)
        in_specs.append(pl.BlockSpec(memory_space=pl.ANY))
    return pl.pallas_call(
        functools.partial(low_kernel, start, modes, wide),
        grid=(pairs // block,),
        in_specs=in_specs,
        out_specs=pl.BlockSpec((2 * block, degrees, count), lambda i: (offset + i, 0, 0)),
        out_shape=jax.ShapeDtypeStruct((slots, degrees, count), jnp.bfloat16),
        input_output_aliases=aliases,
        compiler_params=params(),
        cost_estimate=pl.CostEstimate(
            flops=4 * pairs * degrees * half * count, bytes_accessed=pairs * count * half * 8, transcendentals=0
        ),
        name="low_slots",
    )(*operands)


def on_cores(chip_pairs):
    return [(2 * a + core, 2 * b + core) for a, b in chip_pairs for core in range(2)]


def spread(own, z, chips, down_from, up_to):
    down, up = {0: own}, {0: own}
    for d in range(1, chips):
        pairs = [(t + 1, t) for t in range(down_from, chips - d)]
        down[d] = lax.ppermute(down[d - 1], "lev", on_cores(pairs)) if pairs else None
        pairs = [(t - 1, t) for t in range(d, up_to + 1)]
        up[d] = lax.ppermute(up[d - 1], "lev", on_cores(pairs)) if pairs else None
    blocks = [own]
    for d in range(1, chips):
        above, below = down[d], up[chips - d]
        if above is None or below is None:
            blocks.append(below if above is None else above)
        else:
            blocks.append(jnp.where(z + d < chips, above, below))
    blocks = [jnp.zeros_like(own) if b is None else b for b in blocks]
    return jnp.stack(blocks)


def chunk_sizes(pairs):
    if pairs % 16:
        return [pairs]
    if pairs % 80 == 0:
        return [pairs // 5, 2 * pairs // 5, 2 * pairs // 5]
    return [pairs]


def per_device(grid_gradient, legendre, assign):
    fields, rows, nlon = grid_gradient.shape
    modes = nlon // 2
    slots, degrees, half = legendre.shape
    groups = lax.axis_size("lat")
    chips = lax.axis_size("lev") // 2
    lat_id = lax.axis_index("lat")
    lev_id = lax.axis_index("lev")
    z = lev_id // 2
    pairs = slots // 2
    wide = half // 256 * 256 if half >= 256 else half
    lines = 2 * fields
    assign = assign.astype(jnp.int32)

    chunks, start = [], 0
    for size in chunk_sizes(pairs):
        chunks.append((start, size))
        start += size

    by_group = assign.reshape(groups, pairs, 2)
    listed = jnp.concatenate([by_group[:, s : s + n].reshape(groups * n, 2) for s, n in chunks])
    swapped = listed[:, 0] % 2 == 1
    even_wave = jnp.where(swapped, listed[:, 1], listed[:, 0])
    odd_wave = jnp.where(swapped, listed[:, 0], listed[:, 1])
    both = jnp.stack([even_wave, odd_wave])
    first = (even_wave < odd_wave).astype(jnp.float32)[:, None]
    weight = jnp.where(both == 0, 1.0, 2.0).astype(jnp.float32)[:, :, None]
    turn = 2.0 * math.pi / nlon

    def cos_sin(places, scale):
        angle = (both[:, :, None] * places % nlon).astype(jnp.float32) * turn
        return jnp.stack([jnp.cos(angle) * scale, jnp.sin(angle) * scale], axis=1)

    base = cos_sin(jnp.arange(LANES, dtype=jnp.int32), weight)
    step = cos_sin(jnp.arange(0, modes, LANES, dtype=jnp.int32), 1.0)

    here = jnp.arange(rows, dtype=jnp.int32)
    wanted = jnp.where(lat_id >= groups // 2, rows - 1 - here, here)
    row_order = (here[None, :] == wanted[:, None]).astype(jnp.bfloat16)
    folded = fold_grid(grid_gradient, row_order).reshape(4, fields * rows, modes)

    waves = lax.dynamic_slice(assign, (lat_id * slots,), (slots,))
    info = jnp.stack([lev_id])
    order = column_order(lev_id, chips, lines)
    in_pairs = legendre.reshape(pairs, 2, degrees, half)
    second_high = (waves[0::2] < waves[1::2])[:, None, None]
    high_table = jnp.where(second_high, in_pairs[:, 1], in_pairs[:, 0])
    swap = [(i, i ^ 1) for i in range(2 * chips)]

    out = None
    for s, n in chunks:
        given = lax.ppermute(high_table[s : s + n], "lev", on_cores([(0, 1)]))
        spec = zonal(base, step, first, folded, groups, groups * s, n)
        arrived = lax.all_to_all(spec, "lat", split_axis=0, concat_axis=0, tiled=True)
        low, high = halves(arrived, fields, wide)
        high_mine = spread(high, z, chips, 1, max(chips // 2 - 1, 1))
        low_mine = spread(low, z, chips, 0, chips - 1)
        high_other = lax.ppermute(high_mine, "lev", swap)
        own, back = high_slots(s, modes, wide, info, waves, order, legendre, given, high_mine, high_other)
        back = lax.ppermute(back, "lev", on_cores([(1, 0)]))
        low_other = lax.ppermute(low_mine, "lev", swap)
        out = low_slots(s, modes, wide, info, waves, order, legendre, low_mine, low_other, own, back, out)
    return out


def solution(mesh):
    in_specs = (P("lev", "lat", None), P("lat", "lev", None), P())
    out_specs = P("lat", "lev", None)
    return jax.shard_map(
        per_device, mesh=mesh, in_specs=in_specs, out_specs=out_specs, check_vma=False
    )
```

```python
import functools
import math

import jax
import jax.numpy as jnp
from jax import lax
from jax.experimental import pallas as pl
from jax.experimental.pallas import tpu as pltpu
from jax.sharding import PartitionSpec as P

LANES = 128
VMEM_LIMIT = 48 * 1024 * 1024
MARK = jax.ShapeDtypeStruct((8, LANES), jnp.float32)
MARK_SPEC = pl.BlockSpec((8, LANES), lambda *_: (0, 0))
ANY = pl.BlockSpec(memory_space=pl.ANY)
SMALL = pl.CostEstimate(flops=1000, bytes_accessed=1000, transcendentals=0)


def dot_nt(a, b):
    return lax.dot_general(a, b, (((1,), (1,)), ((), ())), preferred_element_type=jnp.float32)


def params():
    return pltpu.CompilerParams(vmem_limit_bytes=VMEM_LIMIT)


def hi_lo(x):
    hi = x.astype(jnp.bfloat16)
    return hi, (x - hi.astype(jnp.float32)).astype(jnp.bfloat16)


def build_table(start, count, base_ref, step_ref, table_ref):
    for parity in range(2):
        cos0 = base_ref[parity, 0, start : start + count]
        sin0 = base_ref[parity, 1, start : start + count]
        for b in range(step_ref.shape[3]):
            cos1 = step_ref[parity, 0, start : start + count, b : b + 1]
            sin1 = step_ref[parity, 1, start : start + count, b : b + 1]
            both = (cos0 * cos1 - sin0 * sin1, -(sin0 * cos1 + cos0 * sin1))
            for c, table in enumerate(both):
                for part, term in enumerate(hi_lo(table)):
                    at = (2 * part + c) * count
                    table_ref[parity, at : at + count, b * LANES : (b + 1) * LANES] = term


def transform(start, count, first_ref, table_ref, folded, out_ref):
    groups, _, _, pairs, _ = out_ref.shape
    found = []
    for parity in range(2):
        main = dot_nt(table_ref[parity], folded[2 * parity])
        found.append(
            main[: 2 * count] + (main[2 * count :] + dot_nt(table_ref[parity, : 2 * count], folded[2 * parity + 1]))
        )
    first = first_ref[start : start + count] > 0.5
    for c in range(2):
        even, odd = found[0][c * count : (c + 1) * count], found[1][c * count : (c + 1) * count]
        low = jnp.where(first, even, odd).astype(jnp.bfloat16)
        high = jnp.where(first, odd, even).astype(jnp.bfloat16)
        for g in range(groups):
            out_ref[g, 0, c] = low[g * pairs : (g + 1) * pairs]
            out_ref[g, 1, c] = high[g * pairs : (g + 1) * pairs]


def fold_kernel(start, count, group, base_ref, step_ref, first_ref, order_ref, *refs):
    fields, refs = refs[:group], refs[-7:]
    out_ref, folded_refs, mark_ref, table_ref = refs[0], refs[1:5], refs[5], refs[6]
    mark_ref[...] = jnp.zeros_like(mark_ref)
    rows, half = order_ref.shape[0], folded_refs[0].shape[1]

    @pl.when(pl.program_id(0) == 0)
    def _():
        build_table(start, count, base_ref, step_ref, table_ref)

    for f, grid_ref in enumerate(fields):
        near, far = grid_ref[0, :, :half], grid_ref[0, :, half:]
        for parity, folded in enumerate((near + far, near - far)):
            for part, term in enumerate(hi_lo(folded)):
                moved = jnp.dot(order_ref[...], term, preferred_element_type=jnp.float32)
                folded_refs[2 * parity + part][f * rows : (f + 1) * rows] = moved.astype(jnp.bfloat16)
    transform(start, count, first_ref, table_ref, [ref[...] for ref in folded_refs], out_ref)


def fold_and_zonal(base, step, first, order, grid, groups, start, pairs, after):
    fields, rows, nlon = grid.shape
    half = nlon // 2
    group = 4 if fields % 4 == 0 and 4 * rows % LANES == 0 else fields
    count = groups * pairs
    whole = [pl.BlockSpec(a.shape, lambda n, r=a.ndim: (0,) * r) for a in (base, step, first, order)]
    return pl.pallas_call(
        functools.partial(fold_kernel, start, count, group),
        grid=(fields // group,),
        in_specs=whole
        + [pl.BlockSpec((1, rows, nlon), lambda n, f=f: (n * group + f, 0, 0)) for f in range(group)]
        + [ANY] * len(after),
        out_specs=(
            pl.BlockSpec((groups, 2, 2, pairs, group * rows), lambda n: (0, 0, 0, 0, n)),
            *[pl.BlockSpec((group * rows, half), lambda n: (n, 0))] * 4,
            MARK_SPEC,
        ),
        out_shape=(
            jax.ShapeDtypeStruct((groups, 2, 2, pairs, fields * rows), jnp.bfloat16),
            *[jax.ShapeDtypeStruct((fields * rows, half), jnp.bfloat16)] * 4,
            MARK,
        ),
        scratch_shapes=[pltpu.VMEM((2, 4 * count, half), jnp.bfloat16)],
        compiler_params=params(),
        cost_estimate=SMALL,
        name="fold_and_zonal",
    )(base, step, first, order, *[grid] * group, *after)


def zonal_kernel(start, count, base_ref, step_ref, first_ref, *refs):
    folded, (out_ref, mark_ref, table_ref) = refs[:4], refs[-3:]
    mark_ref[...] = jnp.zeros_like(mark_ref)

    @pl.when(pl.program_id(0) == 0)
    def _():
        build_table(start, count, base_ref, step_ref, table_ref)

    transform(start, count, first_ref, table_ref, [ref[...] for ref in folded], out_ref)


def zonal(base, step, first, folded, groups, start, pairs, after):
    columns, half = folded[0].shape
    block = columns // 5 if columns % (5 * LANES) == 0 else columns
    count = groups * pairs
    whole = [pl.BlockSpec(a.shape, lambda n, r=a.ndim: (0,) * r) for a in (base, step, first)]
    return pl.pallas_call(
        functools.partial(zonal_kernel, start, count),
        grid=(columns // block,),
        in_specs=whole + [pl.BlockSpec((block, half), lambda n: (n, 0))] * 4 + [ANY] * len(after),
        out_specs=(pl.BlockSpec((groups, 2, 2, pairs, block), lambda n: (0, 0, 0, 0, n)), MARK_SPEC),
        out_shape=(jax.ShapeDtypeStruct((groups, 2, 2, pairs, columns), jnp.bfloat16), MARK),
        scratch_shapes=[pltpu.VMEM((2, 4 * count, half), jnp.bfloat16)],
        compiler_params=params(),
        cost_estimate=SMALL,
        name="zonal",
    )(base, step, first, *folded, *after)


def halves_kernel(fields, wide, in_ref, *refs):
    both_ref, again_ref, low_ref, mark_ref, work_ref = refs[-5:]
    mark_ref[...] = jnp.zeros_like(mark_ref)
    groups, _, _, pairs, columns = in_ref.shape
    rows = columns // fields
    for which in range(2):
        for c in range(2):
            parts = [in_ref[g, which, c].astype(jnp.float32) for g in range(groups)]
            sums = [parts[g] + parts[groups - 1 - g] for g in range(groups // 2)]
            gaps = [parts[g] - parts[groups - 1 - g] for g in range(groups // 2)]
            for f in range(fields):
                at = slice(f * rows, (f + 1) * rows)
                even = jnp.concatenate([x[:, at] for x in sums], axis=1)
                odd = jnp.concatenate([x[:, at] for x in gaps], axis=1)
                whole = jnp.concatenate([even[:, :wide], odd[:, :wide], even[:, wide:], odd[:, wide:]], axis=1)
                work_ref[:, c * fields + f, :] = whole
        found = work_ref[...].astype(jnp.bfloat16)
        both_ref[which] = found
        again_ref[which] = found
        if which == 0:
            low_ref[...] = found


def halves(arrived, fields, wide, after):
    groups, _, _, pairs, columns = arrived.shape
    shape = (pairs, 2 * fields, groups * columns // fields)
    return pl.pallas_call(
        functools.partial(halves_kernel, fields, wide),
        out_shape=(
            *[jax.ShapeDtypeStruct((2, *shape), jnp.bfloat16)] * 2,
            jax.ShapeDtypeStruct(shape, jnp.bfloat16),
            MARK,
        ),
        in_specs=[pl.BlockSpec(memory_space=pltpu.VMEM)] + [ANY] * len(after),
        out_specs=(pl.BlockSpec(memory_space=pltpu.VMEM),) * 4,
        scratch_shapes=[pltpu.VMEM(shape, jnp.float32)],
        compiler_params=params(),
        cost_estimate=SMALL,
        name="halves",
    )(arrived, *after)


def contract(table, mine, other, index, wide):
    chips, _, lines, length = mine.shape
    spec = jnp.concatenate(
        [ref[d, index] for d in range(chips) for ref in (mine, other)], axis=0
    )
    half = length // 2
    count = spec.shape[0]
    degrees = table.shape[0]
    even_row = lax.rem(lax.broadcasted_iota(jnp.int32, (degrees, 1), 0), 2) == 0
    main = dot_nt(table[:, :wide], jnp.concatenate([spec[:, :wide], spec[:, wide : 2 * wide]], axis=0))
    total = jnp.where(even_row, main[:, :count], main[:, count:])
    if half > wide:
        rest = table[:, wide:].astype(jnp.float32)
        rest = jnp.concatenate([jnp.where(even_row, rest, 0.0), jnp.where(even_row, 0.0, rest)], axis=1)
        total = total + dot_nt(rest.astype(jnp.bfloat16), spec[:, 2 * wide :])
    return total


def keep_valid(values, first_degree, wave, modes):
    degrees = first_degree + lax.broadcasted_iota(jnp.int32, (values.shape[0], 1), 0)
    return jnp.where(degrees < modes - wave, values, 0.0).astype(jnp.bfloat16)


def column_order(lev_id, sources, lines):
    chips = sources.shape[0]
    fields = lines // 2
    count = 2 * chips * lines
    row = jnp.arange(count, dtype=jnp.int32)
    chip = jnp.repeat(sources, 2 * lines)
    core = (row // lines + lev_id) % 2
    c = row // fields % 2
    target = c * (count // 2) + (2 * chip + core) * fields + row % fields
    return (row[None, :] == target[:, None]).astype(jnp.bfloat16)


def in_order(values, order):
    count, degrees, columns = values.shape
    moved = jnp.dot(values.reshape(count * degrees, columns), order, preferred_element_type=jnp.float32)
    return moved.astype(jnp.bfloat16).reshape(count, degrees, columns)


def high_kernel(start, modes, wide, info_ref, waves_ref, order_ref, table_ref, given_ref, mine_ref, other_ref, *refs):
    own_ref, back_ref, mark_ref, work_ref = refs[-4:]
    mark_ref[...] = jnp.zeros_like(mark_ref)
    pairs, degrees, _ = own_ref.shape
    block = pl.program_id(0)
    lev = info_ref[0]
    for i in range(pairs):
        q = start + block * pairs + i
        swapped = waves_ref[2 * q] > waves_ref[2 * q + 1]
        wave = jnp.maximum(waves_ref[2 * q], waves_ref[2 * q + 1])
        table = table_ref[2 * i + jnp.where(swapped, 0, 1)]
        both = jnp.concatenate([table, unpacked(given_ref[i], *table.shape)], axis=0)
        values = contract(both, mine_ref, other_ref, i, wide)
        work_ref[i] = keep_valid(values[:degrees], lev * degrees, wave, modes)
        work_ref[pairs + i] = keep_valid(values[degrees:], (lev - 2) * degrees, wave, modes)
    own_ref[...] = in_order(work_ref[:pairs], order_ref[...])
    back_ref[...] = in_order(work_ref[pairs:], order_ref[...])


def low_kernel(start, modes, wide, info_ref, waves_ref, order_ref, table_ref, mine_ref, other_ref, own_ref, back_ref, *refs):
    out_ref, mark_ref, work_ref = refs[-3:]
    mark_ref[...] = jnp.zeros_like(mark_ref)
    pairs, degrees, _ = own_ref.shape
    block = pl.program_id(0)
    lev = info_ref[0]
    for i in range(pairs):
        q = start + block * pairs + i
        swapped = waves_ref[2 * q] > waves_ref[2 * q + 1]
        wave = jnp.minimum(waves_ref[2 * q], waves_ref[2 * q + 1])
        table = table_ref[2 * i + jnp.where(swapped, 1, 0)]
        values = contract(table, mine_ref, other_ref, i, wide)
        work_ref[i] = keep_valid(values, lev * degrees, wave, modes)
    found = in_order(work_ref[...], order_ref[...])
    for i in range(pairs):
        q = start + block * pairs + i
        swapped = waves_ref[2 * q] > waves_ref[2 * q + 1]
        out_ref[2 * i + jnp.where(swapped, 1, 0)] = found[i]
        out_ref[2 * i + jnp.where(swapped, 0, 1)] = jnp.where(lev < 2, back_ref[i], own_ref[i])


def legendre_specs(start, block, degrees, half, mine, count):
    chips, _, lines, length = mine.shape
    smem = pl.BlockSpec(memory_space=pltpu.SMEM)
    offset = start // block
    piece = pl.BlockSpec((chips, block, lines, length), lambda i: (0, i, 0, 0))
    return [smem, smem, pl.BlockSpec((count, count), lambda i: (0, 0)),
            pl.BlockSpec((2 * block, degrees, half), lambda i: (offset + i, 0, 0))], piece


def block_pairs(start, pairs):
    for size in (8, 4, 2):
        if start % size == 0 and pairs % size == 0:
            return size
    return pairs if start % pairs == 0 else 1


def high_slots(start, modes, wide, info, waves, order, table, given, mine, other, after):
    _, degrees, half = table.shape
    pairs, *line = given.shape
    count = order.shape[0]
    block = block_pairs(start, pairs)
    shared, piece = legendre_specs(start, block, degrees, half, mine, count)
    result = pl.BlockSpec((block, degrees, count), lambda i: (i, 0, 0))
    shape = jax.ShapeDtypeStruct((pairs, degrees, count), jnp.bfloat16)
    return pl.pallas_call(
        functools.partial(high_kernel, start, modes, wide),
        grid=(pairs // block,),
        in_specs=shared + [pl.BlockSpec((block, *line), lambda i: (i, 0, 0)), piece, piece] + [ANY] * len(after),
        out_specs=(result, result, MARK_SPEC),
        out_shape=(shape, shape, MARK),
        scratch_shapes=[pltpu.VMEM((2 * block, degrees, count), jnp.bfloat16)],
        compiler_params=params(),
        cost_estimate=SMALL,
        name="high_slots",
    )(info, waves, order, table, given, mine, other, *after)


def low_slots(start, modes, wide, info, waves, order, table, mine, other, own, back, out, after):
    pairs, degrees, count = own.shape
    slots, _, half = table.shape
    block = block_pairs(start, pairs)
    offset = start // block
    shared, piece = legendre_specs(start, block, degrees, half, mine, count)
    given = pl.BlockSpec((block, degrees, count), lambda i: (i, 0, 0))
    operands = [info, waves, order, table, mine, other, own, back]
    in_specs = shared + [piece, piece, given, given]
    aliases = {}
    if out is not None:
        aliases = {len(operands): 0}
        operands.append(out)
        in_specs.append(ANY)
    operands += after
    in_specs += [ANY] * len(after)
    return pl.pallas_call(
        functools.partial(low_kernel, start, modes, wide),
        grid=(pairs // block,),
        in_specs=in_specs,
        out_specs=(pl.BlockSpec((2 * block, degrees, count), lambda i: (offset + i, 0, 0)), MARK_SPEC),
        out_shape=(jax.ShapeDtypeStruct((slots, degrees, count), jnp.bfloat16), MARK),
        input_output_aliases=aliases,
        scratch_shapes=[pltpu.VMEM((block, degrees, count), jnp.bfloat16)],
        compiler_params=params(),
        cost_estimate=SMALL,
        name="low_slots",
    )(*operands)


def give_kernel(start, waves_ref, table_ref, *refs):
    out_ref, mark_ref = refs[-2:]
    pairs, lines, _ = out_ref.shape
    degrees, half = table_ref.shape[1:]
    mark_ref[...] = jnp.zeros_like(mark_ref)
    for i in range(pairs):
        q = start + pl.program_id(0) * pairs + i
        table = table_ref[2 * i + jnp.where(waves_ref[2 * q] > waves_ref[2 * q + 1], 0, 1)]
        if lines == degrees:
            out_ref[i] = table
            continue
        whole = half // LANES
        for b in range(whole):
            out_ref[i, b * degrees : (b + 1) * degrees] = table[:, b * LANES : (b + 1) * LANES]
        rest = table[:, whole * LANES :]
        out_ref[i, whole * degrees :] = jnp.concatenate([rest[: degrees // 2], rest[degrees // 2 :]], axis=1)


def packs(degrees, half):
    return half % LANES == LANES // 2 and degrees % 16 == 0


def unpacked(block, degrees, half):
    if not packs(degrees, half):
        return block
    whole = half // LANES
    rest = block[whole * degrees :]
    rest = jnp.concatenate([rest[:, : LANES // 2], rest[:, LANES // 2 :]], axis=0)
    return jnp.concatenate([block[b * degrees : (b + 1) * degrees] for b in range(whole)] + [rest], axis=1)


def give(waves, table, start, pairs, after):
    _, degrees, half = table.shape
    block = block_pairs(start, pairs)
    offset = start // block
    line = (degrees * half // LANES, LANES) if packs(degrees, half) else (degrees, half)
    return pl.pallas_call(
        functools.partial(give_kernel, start),
        grid=(pairs // block,),
        in_specs=[
            pl.BlockSpec(memory_space=pltpu.SMEM),
            pl.BlockSpec((2 * block, degrees, half), lambda i: (offset + i, 0, 0)),
        ] + [ANY] * len(after),
        out_specs=(pl.BlockSpec((block, *line), lambda i: (i, 0, 0)), MARK_SPEC),
        out_shape=(jax.ShapeDtypeStruct((pairs, *line), jnp.bfloat16), MARK),
        compiler_params=params(),
        cost_estimate=SMALL,
        name="give",
    )(waves, table, *after)


def gate_kernel(*refs):
    pass


def gate(arrays, after):
    count = len(arrays)
    found = pl.pallas_call(
        gate_kernel,
        in_specs=[ANY] * (count + len(after)),
        out_specs=(ANY,) * (count + 1),
        out_shape=(*[jax.ShapeDtypeStruct(a.shape, a.dtype) for a in arrays], MARK),
        input_output_aliases={i: i for i in range(count)},
        compiler_params=params(),
        cost_estimate=SMALL,
        name="gate",
    )(*arrays, *after)
    return found[:count], found[count]


def on_cores(chip_pairs):
    return [(2 * a + core, 2 * b + core) for a, b in chip_pairs for core in range(2)]


def send(block, pairs):
    return lax.ppermute(block, "lev", on_cores(pairs))


class Links:
    def __init__(self):
        self.mark = ()

    def send(self, block, pairs, after=()):
        after = tuple(mark for mark in after if mark is not None)
        if self.mark or after:
            (block,), _ = gate([block], (*self.mark, *after))
        (there,), mark = gate([send(block, pairs)], ())
        self.mark = (mark,)
        return block, there, mark


INWARD = [(0, 1), (3, 2)]
CENTRE = [(1, 2), (2, 1)]
OUTWARD = [(1, 0), (2, 3)]
GIVE = [(0, 1)]
RETURN = [(1, 0)]


def chunk_sizes(pairs):
    if pairs % 80 == 0:
        return [pairs // 5, 2 * pairs // 5, 2 * pairs // 5]
    return [pairs]


def laid_out(sizes):
    found, start = [], 0
    for size in sizes:
        found.append((start, size))
        start += size
    return found


def given_parts(sizes):
    beside = [8 * max(3 * size // 32, min(size // 8, 2)) for size in sizes]
    return laid_out([sum(sizes) - sum(beside)] + beside)


def per_device(grid_gradient, legendre, assign):
    fields, rows, nlon = grid_gradient.shape
    modes = nlon // 2
    slots, degrees, half = legendre.shape
    groups = lax.axis_size("lat")
    chips = lax.axis_size("lev") // 2
    lat_id = lax.axis_index("lat")
    lev_id = lax.axis_index("lev")
    z = lev_id // 2
    pairs = slots // 2
    wide = half // 256 * 256 if half >= 256 else half
    lines = 2 * fields
    in_line = chips == 4
    sizes = chunk_sizes(pairs) if in_line else [pairs]
    chunks = laid_out(sizes)
    count = len(chunks)
    assign = assign.astype(jnp.int32)

    by_group = assign.reshape(groups, pairs, 2)
    listed = jnp.concatenate([by_group[:, s : s + n].reshape(groups * n, 2) for s, n in chunks])
    swapped = listed[:, 0] % 2 == 1
    even_wave = jnp.where(swapped, listed[:, 1], listed[:, 0])
    odd_wave = jnp.where(swapped, listed[:, 0], listed[:, 1])
    waves_of = jnp.stack([even_wave, odd_wave])
    first = (even_wave < odd_wave).astype(jnp.float32)[:, None]
    weight = jnp.where(waves_of == 0, 1.0, 2.0).astype(jnp.float32)[:, :, None]
    turn = 2.0 * math.pi / nlon

    def cos_sin(places, scale):
        angle = (waves_of[:, :, None] * places % nlon).astype(jnp.float32) * turn
        return jnp.stack([jnp.cos(angle) * scale, jnp.sin(angle) * scale], axis=1)

    base = cos_sin(jnp.arange(LANES, dtype=jnp.int32), weight)
    step = cos_sin(jnp.arange(0, modes, LANES, dtype=jnp.int32), 1.0)

    here = jnp.arange(rows, dtype=jnp.int32)
    wanted = jnp.where(lat_id >= groups // 2, rows - 1 - here, here)
    row_order = (here[None, :] == wanted[:, None]).astype(jnp.bfloat16)

    waves = lax.dynamic_slice(assign, (lat_id * slots,), (slots,))
    info = jnp.stack([lev_id])
    spec, zonal_mark = [None] * count, [None] * count
    state = {"mark": (), "out": None}

    def do_zonal(i):
        s, n = chunks[i]
        if i == 0:
            found, *state["folded"], mark = fold_and_zonal(
                base, step, first, row_order, grid_gradient, groups, groups * s, n, ()
            )
        else:
            found, mark = zonal(base, step, first, state["folded"], groups, groups * s, n, state["mark"])
        state["mark"] = (mark,)
        zonal_mark[i] = mark
        spec[i] = lax.all_to_all(found, "lat", split_axis=0, concat_axis=0, tiled=True)

    def do_halves(i):
        both, again, low, mark = halves(spec[i], fields, wide, state["mark"])
        state["mark"] = (mark,)
        return both, again, low, mark

    if not in_line:
        do_zonal(0)
        both, _, _, _ = do_halves(0)
        everyone = lax.all_gather(both, "lev", axis=0)
        order = column_order(0, jnp.arange(chips), lines)
        given = jnp.zeros((pairs, degrees, half), jnp.bfloat16)
        own, _, _ = high_slots(
            0, modes, wide, info, waves, order, legendre, given, everyone[0::2, 1], everyone[1::2, 1], ()
        )
        found, _ = low_slots(
            0, modes, wide, info, waves, order, legendre, everyone[0::2, 0], everyone[1::2, 0], own, own, None, ()
        )
        return found

    inner = (z == 1) | (z == 2)
    sources = jnp.array([[0, 1, 2, 3], [1, 0, 2, 3], [2, 3, 1, 0], [3, 2, 1, 0]], jnp.int32)[z]
    order = column_order(lev_id, sources, lines)
    swap = [(i, i ^ 1) for i in range(2 * chips)]
    parts = given_parts(sizes)
    gives = len(parts)
    ready, table, give_mark, table_mark = [[None] * gives for _ in range(4)]
    both, again, low, halves_mark, own, back, low_mark = [[None] * count for _ in range(7)]
    first_in, first_cross, first_out = [[None] * count for _ in range(3)]
    second_cross, second_out = [[None] * count for _ in range(2)]
    out_mark, out2_mark, out3_mark, back_mark = [[None] * count for _ in range(4)]
    inward, centre, outward = Links(), Links(), Links()

    def at(marks, i):
        return marks[i] if 0 <= i < len(marks) else None

    def do_give(i):
        if parts[i][1]:
            ready[i], mark = give(waves, legendre, *parts[i], state["mark"])
            state["mark"] = (mark,)
            give_mark[i] = mark

    def send_table(i):
        if ready[i] is not None:
            _, table[i], table_mark[i] = inward.send(ready[i], GIVE)

    def given_for(i):
        s, n = chunks[i]
        found = []
        for (start, size), block in zip(parts, table):
            low_end, high_end = max(s, start), min(s + n, start + size)
            if low_end < high_end:
                found.append(block[low_end - start : high_end - start])
        return jnp.concatenate(found)

    def send_in(i):
        again[i], first_in[i], _ = inward.send(again[i], INWARD)

    def send_cross(i):
        after = (at(out2_mark, i - 1), at(back_mark, i - 2), at(table_mark, i), at(zonal_mark, i + 1))
        both[i], first_cross[i], _ = centre.send(both[i], CENTRE, after)

    def send_out(i):
        low[i], first_out[i], out_mark[i] = outward.send(low[i], OUTWARD)

    def send_cross2(i):
        after = (at(out_mark, i), at(out3_mark, i - 1), at(low_mark, i - 2))
        if i == 0:
            after += (at(give_mark, 1),)
        else:
            after += (at(give_mark, i + 1), at(halves_mark, i + 1))
        first_in[i], second_cross[i], _ = centre.send(first_in[i], CENTRE, after)

    def send_out2(i):
        _, second_out[i], out2_mark[i] = outward.send(first_cross[i][0], OUTWARD)

    def send_out3(i):
        _, third, out3_mark[i] = outward.send(
            second_cross[i][0], OUTWARD, (at(low_mark, i - 2), at(table_mark, i + 1) if i == count - 1 else None)
        )
        pieces = [low[i]]
        for passed, came in ((first_in, first_out[i]), (first_cross, second_out[i]), (second_cross, third)):
            pieces.append(jnp.where(inner, passed[i][0], came))
        low[i] = jnp.stack(pieces)

    def do_high(i):
        mine = jnp.stack([passed[i][1] for passed in (both, first_in, first_cross, second_cross)])
        own[i], back[i], _ = high_slots(
            chunks[i][0], modes, wide, info, waves, order, legendre, given_for(i), mine,
            lax.ppermute(mine, "lev", swap), (),
        )

    def send_back(i):
        _, back[i], back_mark[i] = outward.send(back[i], RETURN)

    def do_low(i):
        state["out"], low_mark[i] = low_slots(
            chunks[i][0], modes, wide, info, waves, order, legendre, low[i], lax.ppermute(low[i], "lev", swap), own[i],
            back[i], state["out"], (),
        )

    do_zonal(0)
    do_give(0)
    send_table(0)
    if count > 1:
        do_zonal(1)
    both[0], again[0], low[0], halves_mark[0] = do_halves(0)
    send_in(0)
    send_cross(0)
    send_out(0)
    for i in range(count):
        do_give(i + 1)
        send_table(i + 1)
        if i + 1 < count:
            both[i + 1], again[i + 1], low[i + 1], halves_mark[i + 1] = do_halves(i + 1)
        if i + 2 < count:
            do_zonal(i + 2)
        send_out2(i)
        if i + 1 < count:
            send_in(i + 1)
        if i > 0:
            do_high(i - 1)
            send_back(i - 1)
            do_low(i - 1)
        send_cross2(i)
        if i + 1 < count:
            send_cross(i + 1)
        send_out3(i)
        if i + 1 < count:
            send_out(i + 1)
    do_high(count - 1)
    send_back(count - 1)
    do_low(count - 1)
    return state["out"]


def solution(mesh):
    in_specs = (P("lev", "lat", None), P("lat", "lev", None), P())
    out_specs = P("lat", "lev", None)
    return jax.shard_map(
        per_device, mesh=mesh, in_specs=in_specs, out_specs=out_specs, check_vma=False
    )
```

```python
import functools
import math

import jax
import jax.numpy as jnp
from jax import lax
from jax.experimental import pallas as pl
from jax.experimental.pallas import tpu as pltpu
from jax.sharding import PartitionSpec as P

LANES = 128
VMEM_LIMIT = 48 * 1024 * 1024
MARK = jax.ShapeDtypeStruct((8, LANES), jnp.float32)
MARK_SPEC = pl.BlockSpec((8, LANES), lambda *_: (0, 0))
ANY = pl.BlockSpec(memory_space=pl.ANY)
SMALL = pl.CostEstimate(flops=1000, bytes_accessed=1000, transcendentals=0)


def dot_nt(a, b):
    return lax.dot_general(a, b, (((1,), (1,)), ((), ())), preferred_element_type=jnp.float32)


def params():
    return pltpu.CompilerParams(vmem_limit_bytes=VMEM_LIMIT)


def hi_lo(x):
    hi = x.astype(jnp.bfloat16)
    return hi, (x - hi.astype(jnp.float32)).astype(jnp.bfloat16)


def build_table(start, count, base_ref, step_ref, table_ref):
    for parity in range(2):
        cos0 = base_ref[parity, 0, start : start + count]
        sin0 = base_ref[parity, 1, start : start + count]
        for b in range(step_ref.shape[3]):
            cos1 = step_ref[parity, 0, start : start + count, b : b + 1]
            sin1 = step_ref[parity, 1, start : start + count, b : b + 1]
            both = (cos0 * cos1 - sin0 * sin1, -(sin0 * cos1 + cos0 * sin1))
            for c, table in enumerate(both):
                for part, term in enumerate(hi_lo(table)):
                    at = (2 * part + c) * count
                    table_ref[parity, at : at + count, b * LANES : (b + 1) * LANES] = term


def transform(start, sizes, first_ref, table_ref, folded, out_ref):
    groups = out_ref.shape[0]
    count = groups * sum(sizes)
    found = []
    for parity in range(2):
        main = dot_nt(table_ref[parity], folded[2 * parity])
        found.append(
            main[: 2 * count] + (main[2 * count :] + dot_nt(table_ref[parity, : 2 * count], folded[2 * parity + 1]))
        )
    first = first_ref[start : start + count] > 0.5
    chosen = []
    for left, right in (found, found[::-1]):
        for c in range(2):
            at = slice(c * count, (c + 1) * count)
            chosen.append(jnp.where(first, left[at], right[at]))
    for g in range(groups):
        rows, ahead = [], 0
        for pairs in sizes:
            rows += [values[ahead + g * pairs : ahead + (g + 1) * pairs] for values in chosen]
            ahead += groups * pairs
        out_ref[g] = jnp.concatenate(rows, axis=0).astype(jnp.bfloat16)


def fold_kernel(start, sizes, group, base_ref, step_ref, first_ref, order_ref, *refs):
    fields, refs = refs[:group], refs[-7:]
    out_ref, folded_refs, mark_ref, table_ref = refs[0], refs[1:5], refs[5], refs[6]
    mark_ref[...] = jnp.zeros_like(mark_ref)
    rows, half = order_ref.shape[0], folded_refs[0].shape[1]
    count = out_ref.shape[0] * sum(sizes)

    @pl.when(pl.program_id(0) == 0)
    def _():
        build_table(start, count, base_ref, step_ref, table_ref)

    for f, grid_ref in enumerate(fields):
        near, far = grid_ref[0, :, :half], grid_ref[0, :, half:]
        for parity, folded in enumerate((near + far, near - far)):
            for part, term in enumerate(hi_lo(folded)):
                moved = jnp.dot(order_ref[...], term, preferred_element_type=jnp.float32)
                folded_refs[2 * parity + part][f * rows : (f + 1) * rows] = moved.astype(jnp.bfloat16)
    transform(start, sizes, first_ref, table_ref, [ref[...] for ref in folded_refs], out_ref)


def fold_and_zonal(base, step, first, order, grid, groups, start, sizes, after):
    fields, rows, nlon = grid.shape
    half = nlon // 2
    group = 4 if fields % 4 == 0 and 4 * rows % LANES == 0 else fields
    pairs = sum(sizes)
    count = groups * pairs
    whole = [pl.BlockSpec(a.shape, lambda n, r=a.ndim: (0,) * r) for a in (base, step, first, order)]
    return pl.pallas_call(
        functools.partial(fold_kernel, start, sizes, group),
        grid=(fields // group,),
        in_specs=whole
        + [pl.BlockSpec((1, rows, nlon), lambda n, f=f: (n * group + f, 0, 0)) for f in range(group)]
        + [ANY] * len(after),
        out_specs=(
            pl.BlockSpec((groups, 4 * pairs, group * rows), lambda n: (0, 0, n)),
            *[pl.BlockSpec((group * rows, half), lambda n: (n, 0))] * 4,
            MARK_SPEC,
        ),
        out_shape=(
            jax.ShapeDtypeStruct((groups, 4 * pairs, fields * rows), jnp.bfloat16),
            *[jax.ShapeDtypeStruct((fields * rows, half), jnp.bfloat16)] * 4,
            MARK,
        ),
        scratch_shapes=[pltpu.VMEM((2, 4 * count, half), jnp.bfloat16)],
        compiler_params=params(),
        cost_estimate=SMALL,
        name="fold_and_zonal",
    )(base, step, first, order, *[grid] * group, *after)


def zonal_kernel(start, sizes, base_ref, step_ref, first_ref, *refs):
    folded, (out_ref, mark_ref, table_ref) = refs[:4], refs[-3:]
    count = out_ref.shape[0] * sum(sizes)
    mark_ref[...] = jnp.zeros_like(mark_ref)

    @pl.when(pl.program_id(0) == 0)
    def _():
        build_table(start, count, base_ref, step_ref, table_ref)

    transform(start, sizes, first_ref, table_ref, [ref[...] for ref in folded], out_ref)


def zonal(base, step, first, folded, groups, start, sizes, after):
    columns, half = folded[0].shape
    block = columns // 5 if columns % (5 * LANES) == 0 else columns
    pairs = sum(sizes)
    count = groups * pairs
    whole = [pl.BlockSpec(a.shape, lambda n, r=a.ndim: (0,) * r) for a in (base, step, first)]
    return pl.pallas_call(
        functools.partial(zonal_kernel, start, sizes),
        grid=(columns // block,),
        in_specs=whole + [pl.BlockSpec((block, half), lambda n: (n, 0))] * 4 + [ANY] * len(after),
        out_specs=(pl.BlockSpec((groups, 4 * pairs, block), lambda n: (0, 0, n)), MARK_SPEC),
        out_shape=(jax.ShapeDtypeStruct((groups, 4 * pairs, columns), jnp.bfloat16), MARK),
        scratch_shapes=[pltpu.VMEM((2, 4 * count, half), jnp.bfloat16)],
        compiler_params=params(),
        cost_estimate=SMALL,
        name="zonal",
    )(base, step, first, *folded, *after)


def halves_kernel(fields, wide, in_ref, *refs):
    both_ref, again_ref, low_ref, mark_ref, work_ref = refs[-5:]
    mark_ref[...] = jnp.zeros_like(mark_ref)
    bands = in_ref.shape[0] // 2
    pairs, lines, length = work_ref.shape
    rows = in_ref.shape[2] // fields
    for which in range(2):
        for core in range(2):
            for c in range(2):
                at = slice((2 * which + c) * pairs, (2 * which + c + 1) * pairs)
                parts = [in_ref[2 * b + core].astype(jnp.float32)[at] for b in range(bands)]
                sums = [parts[b] + parts[bands - 1 - b] for b in range(bands // 2)]
                gaps = [parts[b] - parts[bands - 1 - b] for b in range(bands // 2)]
                for f in range(fields):
                    at = slice(f * rows, (f + 1) * rows)
                    even = jnp.concatenate([x[:, at] for x in sums], axis=1)
                    odd = jnp.concatenate([x[:, at] for x in gaps], axis=1)
                    whole = [even[:, :wide], odd[:, :wide], even[:, wide:], odd[:, wide:]]
                    work_ref[:, (2 * core + c) * fields + f, :] = jnp.concatenate(whole, axis=1)
        for b in range(length // LANES):
            found = work_ref[:, :, b * LANES : (b + 1) * LANES].astype(jnp.bfloat16)
            at = slice(b * lines, (b + 1) * lines)
            both_ref[which, :, at] = found
            again_ref[which, :, at] = found
            if which == 0:
                low_ref[:, at] = found


def halves(arrived, fields, wide, ahead, pairs, after):
    groups, _, columns = arrived.shape
    lines, length = 4 * fields, groups * columns // (2 * fields)
    shape = (pairs, lines * length // LANES, LANES)
    shapes = [(2, *shape), (2, *shape), shape]
    return pl.pallas_call(
        functools.partial(halves_kernel, fields, wide),
        grid=(1,),
        out_shape=(*[jax.ShapeDtypeStruct(each, jnp.bfloat16) for each in shapes], MARK),
        in_specs=[pl.BlockSpec((groups, 4 * pairs, columns), lambda _: (0, ahead // pairs, 0))] + [ANY] * len(after),
        out_specs=(*[pl.BlockSpec(each, lambda _, r=len(each): (0,) * r) for each in shapes], MARK_SPEC),
        scratch_shapes=[pltpu.VMEM((pairs, lines, length), jnp.float32)],
        compiler_params=params(),
        cost_estimate=SMALL,
        name="halves",
    )(arrived, *after)


def whole_lines(block, lines, length):
    tiles = length // LANES
    found = []
    for start in range(0, block.shape[0], tiles * lines):
        found.append(
            jnp.concatenate([block[start + b * lines : start + (b + 1) * lines] for b in range(tiles)], axis=1)
        )
    return found


def contract(table, spec, wide):
    half = spec.shape[1] // 2
    count = spec.shape[0]
    even_row = lax.rem(lax.broadcasted_iota(jnp.int32, (table.shape[0], 1), 0), 2) == 0
    main = dot_nt(table[:, :wide], jnp.concatenate([spec[:, :wide], spec[:, wide : 2 * wide]], axis=0))
    total = jnp.where(even_row, main[:, :count], main[:, count:])
    if half > wide:
        rest = table[:, wide:].astype(jnp.float32)
        rest = jnp.concatenate([jnp.where(even_row, rest, 0.0), jnp.where(even_row, 0.0, rest)], axis=1)
        total = total + dot_nt(rest.astype(jnp.bfloat16), spec[:, 2 * wide :])
    return total


def keep_valid(values, lev, wave, modes):
    degrees = values.shape[0] // 2
    row = lax.broadcasted_iota(jnp.int32, (values.shape[0], 1), 0)
    other = lev + 1 - 2 * lax.rem(lev, 2)
    degree = jnp.where(row < degrees, lev * degrees + row, other * degrees + row - degrees)
    return jnp.where(degree < modes - wave, values, 0.0).astype(jnp.bfloat16)


def column_order(sources, fields):
    count = sources.shape[0] * 4 * fields
    row = jnp.arange(count, dtype=jnp.int32)
    chip = jnp.repeat(sources, 4 * fields)
    core = row // (2 * fields) % 2
    c = row // fields % 2
    target = c * (count // 2) + (2 * chip + core) * fields + row % fields
    return (row[None, :] == target[:, None]).astype(jnp.bfloat16)


def in_order(values, order):
    count, degrees, columns = values.shape
    moved = jnp.dot(values.reshape(count * degrees, columns), order, preferred_element_type=jnp.float32)
    return moved.astype(jnp.bfloat16).reshape(count, degrees, columns)


def chip_table(own_ref, other_ref, slot):
    return jnp.concatenate([own_ref[slot], other_ref[slot]], axis=0)


def pair_of(waves_ref, q):
    left, right = waves_ref[2 * q], waves_ref[2 * q + 1]
    return left > right, jnp.minimum(left, right), jnp.maximum(left, right)


def high_kernel(parts, ends, lines, start, modes, wide, info_ref, waves_ref, order_ref, own_ref, other_ref, *refs):
    pieces, (kept_ref, sent_ref, sent_back_ref, mark_ref, work_ref) = refs[:parts], refs[-5:]
    given = refs[parts : parts + len(ends)]
    mark_ref[...] = jnp.zeros_like(mark_ref)
    _, pairs, degrees, _ = kept_ref.shape
    lev = info_ref[0]
    for i in range(pairs):
        swapped, _, wave = pair_of(waves_ref, start + pl.program_id(0) * pairs + i)
        table = chip_table(own_ref, other_ref, 2 * i + jnp.where(swapped, 0, 1))
        block = given[-1][i]
        for ref, end in zip(given[-2::-1], ends[-2::-1]):
            block = jnp.where(pl.program_id(0) < end, ref[i], block)
        both = jnp.concatenate([table, unpacked(block, *table.shape)], axis=0)
        spec = sum([whole_lines(piece[i], lines, 2 * table.shape[1]) for piece in pieces], [])
        values = contract(both, jnp.concatenate(spec, axis=0), wide)
        work_ref[i] = keep_valid(values[: 2 * degrees], lev, wave, modes)
        work_ref[pairs + i] = keep_valid(values[2 * degrees :], lev - 2, wave, modes)
    for which in range(2):
        found = in_order(work_ref[which * pairs : (which + 1) * pairs], order_ref[...])
        kept_ref[which] = found[:, :degrees]
        (sent_ref, sent_back_ref)[which][...] = found[:, degrees:]


def low_kernel(parts, lines, start, modes, wide, info_ref, waves_ref, order_ref, own_ref, other_ref, *refs):
    mine, passed, came = refs[0], refs[1 : 1 + parts], refs[1 + parts : 1 + 2 * parts]
    kept_ref, sent_ref, mark_ref, work_ref = refs[-4:]
    mark_ref[...] = jnp.zeros_like(mark_ref)
    pairs, degrees, _ = kept_ref.shape
    lev = info_ref[0]
    for i in range(pairs):
        swapped, wave, _ = pair_of(waves_ref, start + pl.program_id(0) * pairs + i)
        table = chip_table(own_ref, other_ref, 2 * i + jnp.where(swapped, 1, 0))
        pieces = [mine[i]] + [a[i] + b[i] for a, b in zip(passed, came)]
        spec = sum([whole_lines(piece, lines, 2 * table.shape[1]) for piece in pieces], [])
        work_ref[i] = keep_valid(contract(table, jnp.concatenate(spec, axis=0), wide), lev, wave, modes)
    found = in_order(work_ref[...], order_ref[...])
    kept_ref[...], sent_ref[...] = found[:, :degrees], found[:, degrees:]


def finish_kernel(start, info_ref, waves_ref, *refs):
    out_ref, mark_ref = refs[-2:]
    mark_ref[...] = jnp.zeros_like(mark_ref)
    pairs = refs[0].shape[0]
    core = lax.rem(info_ref[0], 2)
    first = info_ref[0] < 2
    for side, (low, high, back) in enumerate((refs[:3], refs[3:6])):
        half = core if side == 0 else 1 - core
        for i in range(pairs):
            q = start + pl.program_id(0) * pairs + i
            swapped = waves_ref[half, 2 * q] > waves_ref[half, 2 * q + 1]
            out_ref[half, 2 * i + jnp.where(swapped, 1, 0)] = low[i]
            out_ref[half, 2 * i + jnp.where(swapped, 0, 1)] = jnp.where(first, back[i], high[i])


def block_pairs(start, pairs):
    for size in (8, 4, 2):
        if start % size == 0 and pairs % size == 0:
            return size
    return pairs if start % pairs == 0 else 1


def over_pairs(kernel, name, steps, info, waves, operands, in_specs, outs, out_specs, scratch=(), alias=None, after=()):
    operands = [*operands, *after]
    in_specs = [*in_specs, *[ANY] * len(after)]
    return pl.pallas_call(
        kernel,
        grid_spec=pltpu.PrefetchScalarGridSpec(
            num_scalar_prefetch=2,
            grid=(steps,),
            in_specs=in_specs,
            out_specs=(*out_specs, pl.BlockSpec((8, LANES), lambda *_: (0, 0))),
            scratch_shapes=list(scratch),
        ),
        out_shape=(*outs, MARK),
        input_output_aliases={} if alias is None else {2 + alias: 0},
        compiler_params=params(),
        cost_estimate=SMALL,
        name=name,
    )(info, waves, *operands)


def table_specs(start, block, table):
    slots, degrees, half = table.shape
    ahead = slots // 2 // (2 * block)
    offset = start // block
    place = lambda i, info, _: (lax.rem(info[0], 2) * ahead + offset + i, 0, 0)
    return [pl.BlockSpec((2 * block, degrees, half), place)] * 2


class Piece:
    def __init__(self, array, ahead=0, which=None):
        self.array, self.ahead, self.which = array, ahead, which

    def spec(self, block):
        shape = self.array.shape[-2:]
        offset, which = self.ahead // block, self.which
        last = self.array.shape[-3] // block - 1
        if which is None:
            return pl.BlockSpec((block, *shape), lambda i, *_: (jnp.clip(offset + i, 0, last), 0, 0))
        return pl.BlockSpec((None, block, *shape), lambda i, *_: (which, jnp.clip(offset + i, 0, last), 0, 0))


def give_kernel(start, info_ref, waves_ref, own_ref, other_ref, *refs):
    out_ref, mark_ref = refs[-2:]
    pairs, lines, _ = out_ref.shape
    mark_ref[...] = jnp.zeros_like(mark_ref)
    for i in range(pairs):
        swapped, _, _ = pair_of(waves_ref, start + pl.program_id(0) * pairs + i)
        table = chip_table(own_ref, other_ref, 2 * i + jnp.where(swapped, 0, 1))
        rows, half = table.shape
        if not packs(rows, half):
            out_ref[i] = table
            continue
        whole = half // LANES
        for b in range(whole):
            out_ref[i, b * rows : (b + 1) * rows] = table[:, b * LANES : (b + 1) * LANES]
        rest = table[:, whole * LANES :]
        out_ref[i, whole * rows :] = jnp.concatenate([rest[: rows // 2], rest[rows // 2 :]], axis=1)


def packs(rows, half):
    return half % LANES == LANES // 2 and rows % 32 == 0


def unpacked(block, rows, half):
    if not packs(rows, half):
        return block
    whole = half // LANES
    rest = block[whole * rows :]
    rest = jnp.concatenate([rest[:, : LANES // 2], rest[:, LANES // 2 :]], axis=0)
    return jnp.concatenate([block[b * rows : (b + 1) * rows] for b in range(whole)] + [rest], axis=1)


def gate_kernel(*refs):
    pass


def gate(arrays, after):
    count = len(arrays)
    found = pl.pallas_call(
        gate_kernel,
        in_specs=[ANY] * (count + len(after)),
        out_specs=(ANY,) * (count + 1),
        out_shape=(*[jax.ShapeDtypeStruct(a.shape, a.dtype) for a in arrays], MARK),
        input_output_aliases={i: i for i in range(count)},
        compiler_params=params(),
        cost_estimate=SMALL,
        name="gate",
    )(*arrays, *after)
    return found[:count], found[count]


def on_cores(chip_pairs):
    return [(2 * a + core, 2 * b + core) for a, b in chip_pairs for core in range(2)]


def send(block, pairs):
    return lax.ppermute(block, "lev", on_cores(pairs))


class Links:
    def __init__(self):
        self.mark = ()

    def send(self, block, pairs, after=(), meanwhile=()):
        after = tuple(mark for mark in after if mark is not None)
        if self.mark or after:
            (block,), _ = gate([block], (*self.mark, *after))
        (there,), mark = gate([send(block, pairs)], tuple(mark for mark in meanwhile if mark is not None))
        self.mark = (mark,)
        return block, there, mark


INWARD = [(0, 1), (3, 2)]
CENTRE = [(1, 2), (2, 1)]
OUTWARD = [(1, 0), (2, 3)]
GIVE = [(0, 1)]
RETURN = [(1, 0)]
SOURCES = [[0, 1, 2, 3], [1, 0, 2, 3], [2, 3, 1, 0], [3, 2, 1, 0]]


def chunk_sizes(pairs):
    if pairs % 40 == 0:
        return [pairs // 5, 2 * pairs // 5, 2 * pairs // 5]
    return [pairs]


def laid_out(sizes):
    found, start = [], 0
    for size in sizes:
        found.append((start, size))
        start += size
    return found


def given_parts(sizes):
    pairs = sum(sizes)
    if len(sizes) == 3 and pairs % 40 == 0:
        return laid_out([pairs // 5, pairs // 5, 2 * pairs // 5, pairs // 5])
    return laid_out([pairs] + [0] * len(sizes))


def per_device(grid_gradient, legendre, assign):
    fields, rows, nlon = grid_gradient.shape
    modes = nlon // 2
    slots, degrees, half = legendre.shape
    bands = lax.axis_size("lat")
    levels = lax.axis_size("lev")
    chips = levels // 2
    lat_id = lax.axis_index("lat")
    lev_id = lax.axis_index("lev")
    z, core = lev_id // 2, lev_id % 2
    groups = 2 * bands
    pairs = slots // 4
    wide = half // 256 * 256 if half >= 256 else half
    in_line = chips == 4
    sizes = chunk_sizes(pairs) if in_line else [pairs]
    chunks = laid_out(sizes)
    count = len(chunks)
    assign = assign.astype(jnp.int32)

    by_group = assign.reshape(groups, pairs, 2)
    listed = jnp.concatenate([by_group[:, s : s + n].reshape(groups * n, 2) for s, n in chunks])
    swapped = listed[:, 0] % 2 == 1
    even_wave = jnp.where(swapped, listed[:, 1], listed[:, 0])
    odd_wave = jnp.where(swapped, listed[:, 0], listed[:, 1])
    waves_of = jnp.stack([even_wave, odd_wave])
    first = (even_wave < odd_wave).astype(jnp.float32)[:, None]
    weight = jnp.where(waves_of == 0, 1.0, 2.0).astype(jnp.float32)[:, :, None]
    turn = 2.0 * math.pi / nlon

    def cos_sin(places, scale):
        angle = (waves_of[:, :, None] * places % nlon).astype(jnp.float32) * turn
        return jnp.stack([jnp.cos(angle) * scale, jnp.sin(angle) * scale], axis=1)

    base = cos_sin(jnp.arange(LANES, dtype=jnp.int32), weight)
    step = cos_sin(jnp.arange(0, modes, LANES, dtype=jnp.int32), 1.0)

    here = jnp.arange(rows, dtype=jnp.int32)
    wanted = jnp.where(lat_id >= bands // 2, rows - 1 - here, here)
    row_order = (here[None, :] == wanted[:, None]).astype(jnp.bfloat16)

    group_waves = lax.dynamic_slice(assign, (lat_id * slots,), (slots,)).reshape(2, slots // 2)
    waves = lax.dynamic_slice(group_waves, (core, 0), (1, slots // 2))[0]
    info = jnp.stack([lev_id])
    swap = [(i, i ^ 1) for i in range(levels)]
    squares = [[b * levels + 2 * chip + side for b in range(bands) for side in range(2)] for chip in range(chips)]
    other_table = lax.ppermute(legendre, "lev", swap)
    spec = {}
    state = {"mark": (), "out": None}

    def exchange(found):
        return lax.all_to_all(
            found, ("lat", "lev"), split_axis=0, concat_axis=0, axis_index_groups=squares, tiled=True
        )

    def zonal_first():
        found, *state["folded"], mark = fold_and_zonal(
            base, step, first, row_order, grid_gradient, groups, 0, sizes[:1], ()
        )
        state["mark"] = (mark,)
        spec[0] = (exchange(found), 0)

    def zonal_rest():
        found, mark = zonal(
            base, step, first, state["folded"], groups, groups * sizes[0], tuple(sizes[1:]), state["mark"]
        )
        state["mark"] = (mark,)
        arrived = exchange(found)
        for i in range(1, count):
            spec[i] = (arrived, chunks[i][0] - sizes[0])

    def do_halves(i):
        arrived, ahead = spec[i]
        both, again, low, mark = halves(arrived, fields, wide, ahead, sizes[i], state["mark"])
        state["mark"] = (mark,)
        return both, again, low, mark

    columns = chips * 4 * fields
    order_spec = pl.BlockSpec((columns, columns), lambda *_: (0, 0))

    lines = 4 * fields

    def high_slots(i, given, ends, pieces):
        s, n = chunks[i]
        block = block_pairs(s, n)
        shape = jax.ShapeDtypeStruct((n, degrees, columns), jnp.bfloat16)
        result = pl.BlockSpec((block, degrees, columns), lambda j, *_: (j, 0, 0))
        shape2 = jax.ShapeDtypeStruct((2, n, degrees, columns), jnp.bfloat16)
        result2 = pl.BlockSpec((2, block, degrees, columns), lambda j, *_: (0, j, 0, 0))
        parts = [*pieces, *given]
        return over_pairs(
            functools.partial(high_kernel, len(pieces), ends, lines, s, modes, wide), "high_slots", n // block, info,
            waves, [order, legendre, other_table, *[piece.array for piece in parts]],
            [order_spec, *table_specs(s, block, legendre), *[piece.spec(block) for piece in parts]],
            (shape2, shape, shape), (result2, result, result),
            [pltpu.VMEM((2 * block, 2 * degrees, columns), jnp.bfloat16)],
        )

    def low_slots(i, mine, passed, came):
        s, n = chunks[i]
        block = block_pairs(s, n)
        shape = jax.ShapeDtypeStruct((n, degrees, columns), jnp.bfloat16)
        result = pl.BlockSpec((block, degrees, columns), lambda j, *_: (j, 0, 0))
        parts = [mine, *passed, *came]
        return over_pairs(
            functools.partial(low_kernel, len(passed), lines, s, modes, wide), "low_slots", n // block, info, waves,
            [order, legendre, other_table, *[piece.array for piece in parts]],
            [order_spec, *table_specs(s, block, legendre), *[piece.spec(block) for piece in parts]],
            (shape, shape), (result, result),
            [pltpu.VMEM((block, 2 * degrees, columns), jnp.bfloat16)],
        )

    def finish(i, kept, got):
        s, n = chunks[i]
        block = block_pairs(s, n)
        before = () if state["out"] is None else (state["out"],)
        parts = [*kept, *got]
        state["out"], mark = over_pairs(
            functools.partial(finish_kernel, s), "finish", n // block, info, group_waves,
            [*[piece.array for piece in parts], *before],
            [*[piece.spec(block) for piece in parts], *[ANY] * len(before)],
            (jax.ShapeDtypeStruct((2, slots // 2, degrees, columns), jnp.bfloat16),),
            (pl.BlockSpec((2, 2 * block, degrees, columns), lambda j, *_: (0, s // block + j, 0, 0)),),
            alias=6 if before else None,
        )
        return mark

    if not in_line:
        zonal_first()
        both, _, _, _ = do_halves(0)
        sides = [[2 * chip + side for chip in range(chips)] for side in range(2)]
        everyone = lax.all_gather(both, "lev", axis=2, axis_index_groups=sides, tiled=True)
        order = column_order(jnp.arange(chips, dtype=jnp.int32), fields)
        given = Piece(jnp.zeros((pairs, 2 * degrees, half), jnp.bfloat16))
        high, sent, _, _ = high_slots(0, [given], [1], [Piece(everyone, 0, 1)])
        got_high = Piece(lax.ppermute(sent, "lev", swap))
        high = Piece(high, 0, 0)
        low, sent, _ = low_slots(0, Piece(everyone, 0, 0), [], [])
        got_low = Piece(lax.ppermute(sent, "lev", swap))
        finish(0, [Piece(low), high, high], [got_low, got_high, got_high])
        return state["out"].reshape(slots, degrees, columns)

    sources = jnp.array(SOURCES, jnp.int32)[z]
    order = column_order(sources, fields)
    parts = given_parts(sizes)
    gives = len(parts)
    ready, table, give_mark, table_mark = [[None] * gives for _ in range(4)]
    both, again, low, halves_mark = [[None] * count for _ in range(4)]
    high, got_high, high_mark, found_low, got_low, low_mark, back, returned = [[None] * count for _ in range(8)]
    first_in, first_cross, second_cross = [[None] * count for _ in range(3)]
    first_out, second_out, third_out = [[None] * count for _ in range(3)]
    in_mark, out_mark, out2_mark, out3_mark = [[None] * count for _ in range(4)]
    inward, centre, outward = Links(), Links(), Links()
    last = count - 1

    def at(marks, i):
        return marks[i] if 0 <= i < len(marks) else None

    def do_give(i):
        s, n = parts[i] if i < gives else (0, 0)
        if n:
            block = block_pairs(s, n)
            line = (2 * degrees * half // LANES, LANES) if packs(2 * degrees, half) else (2 * degrees, half)
            ready[i], give_mark[i] = over_pairs(
                functools.partial(give_kernel, s), "give", n // block, info, waves, [legendre, other_table],
                table_specs(s, block, legendre), (jax.ShapeDtypeStruct((n, *line), jnp.bfloat16),),
                (pl.BlockSpec((block, *line), lambda j, *_: (j, 0, 0)),), after=state["mark"],
            )
            state["mark"] = (give_mark[i],)

    def send_table(i):
        if ready[i] is not None:
            _, table[i], table_mark[i] = inward.send(ready[i], GIVE)

    def prepare(i):
        both[i], again[i], low[i], halves_mark[i] = do_halves(i)

    def send_in(i):
        again[i], first_in[i], in_mark[i] = inward.send(again[i], INWARD)

    def send_cross(i):
        after = (at(out3_mark, i - 2),)
        meanwhile = (at(high_mark, i - 1), at(give_mark, i + 1), at(halves_mark, i + 1) if i else None)
        both[i], first_cross[i], _ = centre.send(both[i], CENTRE, after, meanwhile)

    def send_cross2(i):
        after = (at(out2_mark, i - 1),)
        meanwhile = (at(halves_mark, 1) if i == 0 else None, at(low_mark, i - 1))
        first_in[i], second_cross[i], _ = centre.send(first_in[i], CENTRE, after, meanwhile)

    def send_out():
        low[0], found, out_mark[0] = outward.send(low[0], OUTWARD)
        first_out[0] = Piece(found)

    def send_out2(i):
        meanwhile = (at(table_mark, i + 1),) if i == last else ()
        blocks = [first_cross[i][0]]
        if i < last:
            blocks.append(low[i + 1])
        if i > 0:
            blocks.append(returned[i - 1])
        _, found, out2_mark[i] = outward.send(jnp.concatenate(blocks), OUTWARD, (), meanwhile)
        second_out[i] = Piece(found)
        ahead = sizes[i]
        if i < last:
            first_out[i + 1] = Piece(found, ahead)
            ahead += sizes[i + 1]
        if i > 0:
            came_back(i - 1, found, ahead)

    def came_back(i, found, ahead):
        found = found.reshape(2 * found.shape[0], degrees, columns)
        back[i] = [Piece(found, 2 * ahead), Piece(found, 2 * ahead + sizes[i])]

    def do_high(i):
        pieces = [Piece(passed[i], 0, 1) for passed in (both, first_in, first_cross, second_cross)]
        s, n = chunks[i]
        block = block_pairs(s, n)
        given, ends = [], []
        for (start, size), array in zip(parts, table):
            if max(s, start) < min(s + n, start + size):
                given.append(Piece(array, s - start))
                ends.append((start + size - s) // block)
        high[i], sent, sent_back, high_mark[i] = high_slots(i, given, ends, pieces)
        got_high[i] = lax.ppermute(sent, "lev", swap)
        got_back = lax.ppermute(sent_back, "lev", swap)
        returned[i] = jnp.concatenate([high[i][1], got_back]).reshape(second_cross[i].shape[1:])

    def send_out3(i):
        _, found, out3_mark[i] = outward.send(second_cross[i][0], OUTWARD)
        third_out[i] = Piece(found)

    def send_back(i):
        _, found, _ = outward.send(returned[i], RETURN)
        came_back(i, found, 0)

    def do_low(i):
        passed = [Piece(array[i], 0, 0) for array in (first_in, first_cross, second_cross)]
        found_low[i], sent, low_mark[i] = low_slots(
            i, Piece(both[i], 0, 0), passed, [first_out[i], second_out[i], third_out[i]]
        )
        got_low[i] = lax.ppermute(sent, "lev", swap)

    def do_finish(i):
        finish(
            i,
            [Piece(found_low[i]), Piece(high[i], 0, 0), back[i][0]],
            [Piece(got_low[i]), Piece(got_high[i]), back[i][1]],
        )

    zonal_first()
    do_give(0)
    send_table(0)
    if count > 1:
        zonal_rest()
    prepare(0)
    send_in(0)
    do_give(1)
    send_cross(0)
    send_out()
    for i in range(count):
        if i == 0 and count > 1:
            prepare(1)
        send_table(i + 1)
        if i < last:
            send_in(i + 1)
        send_out2(i)
        if i > 0:
            do_low(i - 1)
            do_finish(i - 1)
        send_cross2(i)
        do_high(i)
        do_give(i + 2)
        if i + 2 < count:
            prepare(i + 2)
        if i < last:
            send_cross(i + 1)
        send_out3(i)
    send_back(last)
    do_low(last)
    do_finish(last)
    return state["out"].reshape(slots, degrees, columns)


def solution(mesh):
    in_specs = (P("lev", "lat", None), P("lat", "lev", None), P())
    out_specs = P("lat", "lev", None)
    return jax.shard_map(
        per_device, mesh=mesh, in_specs=in_specs, out_specs=out_specs, check_vma=False
    )
```

```python
import functools
import math

import jax
import jax.numpy as jnp
from jax import lax
from jax.experimental import pallas as pl
from jax.experimental.pallas import tpu as pltpu
from jax.sharding import PartitionSpec as P

LANES = 128
VMEM_LIMIT = 48 * 1024 * 1024
MARK = jax.ShapeDtypeStruct((8, LANES), jnp.float32)
MARK_SPEC = pl.BlockSpec((8, LANES), lambda *_: (0, 0))
ANY = pl.BlockSpec(memory_space=pl.ANY)
SMALL = pl.CostEstimate(flops=1000, bytes_accessed=1000, transcendentals=0)


def dot_nt(a, b):
    return lax.dot_general(a, b, (((1,), (1,)), ((), ())), preferred_element_type=jnp.float32)


def params():
    return pltpu.CompilerParams(vmem_limit_bytes=VMEM_LIMIT)


def hi_lo(x):
    hi = x.astype(jnp.bfloat16)
    return hi, (x - hi.astype(jnp.float32)).astype(jnp.bfloat16)


def build_table(start, count, base_ref, step_ref, table_ref):
    for parity in range(2):
        cos0 = base_ref[parity, 0, start : start + count]
        sin0 = base_ref[parity, 1, start : start + count]
        for b in range(step_ref.shape[3]):
            cos1 = step_ref[parity, 0, start : start + count, b : b + 1]
            sin1 = step_ref[parity, 1, start : start + count, b : b + 1]
            both = (cos0 * cos1 - sin0 * sin1, -(sin0 * cos1 + cos0 * sin1))
            for c, table in enumerate(both):
                for part, term in enumerate(hi_lo(table)):
                    at = (2 * part + c) * count
                    table_ref[parity, at : at + count, b * LANES : (b + 1) * LANES] = term


def transform(start, sizes, first_ref, table_ref, folded, out_ref):
    groups = out_ref.shape[0]
    count = groups * sum(sizes)
    found = []
    for parity in range(2):
        main = dot_nt(table_ref[parity], folded[2 * parity])
        found.append(
            main[: 2 * count] + (main[2 * count :] + dot_nt(table_ref[parity, : 2 * count], folded[2 * parity + 1]))
        )
    first = first_ref[start : start + count] > 0.5
    chosen = []
    for left, right in (found, found[::-1]):
        for c in range(2):
            at = slice(c * count, (c + 1) * count)
            chosen.append(jnp.where(first, left[at], right[at]))
    for g in range(groups):
        rows, ahead = [], 0
        for pairs in sizes:
            rows += [values[ahead + g * pairs : ahead + (g + 1) * pairs] for values in chosen]
            ahead += groups * pairs
        out_ref[g] = jnp.concatenate(rows, axis=0).astype(jnp.bfloat16)


def fold_kernel(start, sizes, group, base_ref, step_ref, first_ref, order_ref, *refs):
    fields, refs = refs[:group], refs[-7:]
    out_ref, folded_refs, mark_ref, table_ref = refs[0], refs[1:5], refs[5], refs[6]
    mark_ref[...] = jnp.zeros_like(mark_ref)
    rows, half = order_ref.shape[0], folded_refs[0].shape[1]
    count = out_ref.shape[0] * sum(sizes)

    @pl.when(pl.program_id(0) == 0)
    def _():
        build_table(start, count, base_ref, step_ref, table_ref)

    for f, grid_ref in enumerate(fields):
        near, far = grid_ref[0, :, :half], grid_ref[0, :, half:]
        for parity, folded in enumerate((near + far, near - far)):
            for part, term in enumerate(hi_lo(folded)):
                moved = jnp.dot(order_ref[...], term, preferred_element_type=jnp.float32)
                folded_refs[2 * parity + part][f * rows : (f + 1) * rows] = moved.astype(jnp.bfloat16)
    transform(start, sizes, first_ref, table_ref, [ref[...] for ref in folded_refs], out_ref)


def fold_and_zonal(base, step, first, order, grid, groups, start, sizes, after):
    fields, rows, nlon = grid.shape
    half = nlon // 2
    group = 4 if fields % 4 == 0 and 4 * rows % LANES == 0 else fields
    pairs = sum(sizes)
    count = groups * pairs
    whole = [pl.BlockSpec(a.shape, lambda n, r=a.ndim: (0,) * r) for a in (base, step, first, order)]
    return pl.pallas_call(
        functools.partial(fold_kernel, start, sizes, group),
        grid=(fields // group,),
        in_specs=whole
        + [pl.BlockSpec((1, rows, nlon), lambda n, f=f: (n * group + f, 0, 0)) for f in range(group)]
        + [ANY] * len(after),
        out_specs=(
            pl.BlockSpec((groups, 4 * pairs, group * rows), lambda n: (0, 0, n)),
            *[pl.BlockSpec((group * rows, half), lambda n: (n, 0))] * 4,
            MARK_SPEC,
        ),
        out_shape=(
            jax.ShapeDtypeStruct((groups, 4 * pairs, fields * rows), jnp.bfloat16),
            *[jax.ShapeDtypeStruct((fields * rows, half), jnp.bfloat16)] * 4,
            MARK,
        ),
        scratch_shapes=[pltpu.VMEM((2, 4 * count, half), jnp.bfloat16)],
        compiler_params=params(),
        cost_estimate=SMALL,
        name="fold_and_zonal",
    )(base, step, first, order, *[grid] * group, *after)


def zonal_kernel(start, sizes, base_ref, step_ref, first_ref, *refs):
    folded, (out_ref, mark_ref, table_ref) = refs[:4], refs[-3:]
    count = out_ref.shape[0] * sum(sizes)
    mark_ref[...] = jnp.zeros_like(mark_ref)

    @pl.when(pl.program_id(0) == 0)
    def _():
        build_table(start, count, base_ref, step_ref, table_ref)

    transform(start, sizes, first_ref, table_ref, [ref[...] for ref in folded], out_ref)


def zonal(base, step, first, folded, groups, start, sizes, after):
    columns, half = folded[0].shape
    block = columns // 5 if columns % (5 * LANES) == 0 else columns
    pairs = sum(sizes)
    count = groups * pairs
    whole = [pl.BlockSpec(a.shape, lambda n, r=a.ndim: (0,) * r) for a in (base, step, first)]
    return pl.pallas_call(
        functools.partial(zonal_kernel, start, sizes),
        grid=(columns // block,),
        in_specs=whole + [pl.BlockSpec((block, half), lambda n: (n, 0))] * 4 + [ANY] * len(after),
        out_specs=(pl.BlockSpec((groups, 4 * pairs, block), lambda n: (0, 0, n)), MARK_SPEC),
        out_shape=(jax.ShapeDtypeStruct((groups, 4 * pairs, columns), jnp.bfloat16), MARK),
        scratch_shapes=[pltpu.VMEM((2, 4 * count, half), jnp.bfloat16)],
        compiler_params=params(),
        cost_estimate=SMALL,
        name="zonal",
    )(base, step, first, *folded, *after)


def halves_kernel(fields, wide, in_ref, *refs):
    both_ref, again_ref, low_ref, mark_ref, work_ref = refs[-5:]
    mark_ref[...] = jnp.zeros_like(mark_ref)
    bands = in_ref.shape[0] // 2
    pairs, lines, length = work_ref.shape
    rows = in_ref.shape[2] // fields
    for which in range(2):
        for core in range(2):
            for c in range(2):
                at = slice((2 * which + c) * pairs, (2 * which + c + 1) * pairs)
                parts = [in_ref[2 * b + core].astype(jnp.float32)[at] for b in range(bands)]
                sums = [parts[b] + parts[bands - 1 - b] for b in range(bands // 2)]
                gaps = [parts[b] - parts[bands - 1 - b] for b in range(bands // 2)]
                for f in range(fields):
                    at = slice(f * rows, (f + 1) * rows)
                    even = jnp.concatenate([x[:, at] for x in sums], axis=1)
                    odd = jnp.concatenate([x[:, at] for x in gaps], axis=1)
                    whole = [even[:, :wide], odd[:, :wide], even[:, wide:], odd[:, wide:]]
                    work_ref[:, (2 * core + c) * fields + f, :] = jnp.concatenate(whole, axis=1)
        for b in range(length // LANES):
            found = work_ref[:, :, b * LANES : (b + 1) * LANES].astype(jnp.bfloat16)
            at = slice(b * lines, (b + 1) * lines)
            both_ref[which, :, at] = found
            again_ref[which, :, at] = found
            if which == 0:
                low_ref[:, at] = found


def halves(arrived, fields, wide, ahead, pairs, after):
    groups, _, columns = arrived.shape
    lines, length = 4 * fields, groups * columns // (2 * fields)
    shape = (pairs, lines * length // LANES, LANES)
    shapes = [(2, *shape), (2, *shape), shape]
    return pl.pallas_call(
        functools.partial(halves_kernel, fields, wide),
        grid=(1,),
        out_shape=(*[jax.ShapeDtypeStruct(each, jnp.bfloat16) for each in shapes], MARK),
        in_specs=[pl.BlockSpec((groups, 4 * pairs, columns), lambda _: (0, ahead // pairs, 0))] + [ANY] * len(after),
        out_specs=(*[pl.BlockSpec(each, lambda _, r=len(each): (0,) * r) for each in shapes], MARK_SPEC),
        scratch_shapes=[pltpu.VMEM((pairs, lines, length), jnp.float32)],
        compiler_params=params(),
        cost_estimate=SMALL,
        name="halves",
    )(arrived, *after)


def whole_lines(block, lines, length):
    tiles = length // LANES
    found = []
    for start in range(0, block.shape[0], tiles * lines):
        found.append(
            jnp.concatenate([block[start + b * lines : start + (b + 1) * lines] for b in range(tiles)], axis=1)
        )
    return found


def contract(table, spec, wide):
    half = spec.shape[1] // 2
    count = spec.shape[0]
    even_row = lax.rem(lax.broadcasted_iota(jnp.int32, (table.shape[0], 1), 0), 2) == 0
    main = dot_nt(table[:, :wide], jnp.concatenate([spec[:, :wide], spec[:, wide : 2 * wide]], axis=0))
    total = jnp.where(even_row, main[:, :count], main[:, count:])
    if half > wide:
        rest = table[:, wide:].astype(jnp.float32)
        rest = jnp.concatenate([jnp.where(even_row, rest, 0.0), jnp.where(even_row, 0.0, rest)], axis=1)
        total = total + dot_nt(rest.astype(jnp.bfloat16), spec[:, 2 * wide :])
    return total


def keep_valid(values, lev, wave, modes):
    degrees = values.shape[0] // 2
    row = lax.broadcasted_iota(jnp.int32, (values.shape[0], 1), 0)
    other = lev + 1 - 2 * lax.rem(lev, 2)
    degree = jnp.where(row < degrees, lev * degrees + row, other * degrees + row - degrees)
    return jnp.where(degree < modes - wave, values, 0.0).astype(jnp.bfloat16)


def column_order(sources, fields):
    count = sources.shape[0] * 4 * fields
    row = jnp.arange(count, dtype=jnp.int32)
    chip = jnp.repeat(sources, 4 * fields)
    core = row // (2 * fields) % 2
    c = row // fields % 2
    target = c * (count // 2) + (2 * chip + core) * fields + row % fields
    return (row[None, :] == target[:, None]).astype(jnp.bfloat16)


def in_order(values, order):
    count, degrees, columns = values.shape
    moved = jnp.dot(values.reshape(count * degrees, columns), order, preferred_element_type=jnp.float32)
    return moved.astype(jnp.bfloat16).reshape(count, degrees, columns)


def chip_table(own_ref, other_ref, slot):
    return jnp.concatenate([own_ref[slot], other_ref[slot]], axis=0)


def pair_of(waves_ref, q):
    left, right = waves_ref[2 * q], waves_ref[2 * q + 1]
    return left > right, jnp.minimum(left, right), jnp.maximum(left, right)


def high_kernel(parts, ends, lines, start, modes, wide, info_ref, waves_ref, order_ref, own_ref, other_ref, *refs):
    pieces, (kept_ref, sent_ref, sent_back_ref, mark_ref, work_ref) = refs[:parts], refs[-5:]
    given = refs[parts : parts + len(ends)]
    mark_ref[...] = jnp.zeros_like(mark_ref)
    _, pairs, degrees, _ = kept_ref.shape
    lev = info_ref[0]
    for i in range(pairs):
        swapped, _, wave = pair_of(waves_ref, start + pl.program_id(0) * pairs + i)
        table = chip_table(own_ref, other_ref, 2 * i + jnp.where(swapped, 0, 1))
        block = given[-1][i]
        for ref, end in zip(given[-2::-1], ends[-2::-1]):
            block = jnp.where(pl.program_id(0) < end, ref[i], block)
        both = jnp.concatenate([table, unpacked(block, *table.shape)], axis=0)
        spec = sum([whole_lines(piece[i], lines, 2 * table.shape[1]) for piece in pieces], [])
        values = contract(both, jnp.concatenate(spec, axis=0), wide)
        work_ref[i] = keep_valid(values[: 2 * degrees], lev, wave, modes)
        work_ref[pairs + i] = keep_valid(values[2 * degrees :], lev - 2, wave, modes)
    for which in range(2):
        found = in_order(work_ref[which * pairs : (which + 1) * pairs], order_ref[...])
        kept_ref[which] = found[:, :degrees]
        (sent_ref, sent_back_ref)[which][...] = found[:, degrees:]


def low_kernel(parts, lines, start, modes, wide, info_ref, waves_ref, order_ref, own_ref, other_ref, *refs):
    mine, passed, came = refs[0], refs[1 : 1 + parts], refs[1 + parts : 1 + 2 * parts]
    kept_ref, sent_ref, mark_ref, work_ref = refs[-4:]
    mark_ref[...] = jnp.zeros_like(mark_ref)
    pairs, degrees, _ = kept_ref.shape
    lev = info_ref[0]
    for i in range(pairs):
        swapped, wave, _ = pair_of(waves_ref, start + pl.program_id(0) * pairs + i)
        table = chip_table(own_ref, other_ref, 2 * i + jnp.where(swapped, 1, 0))
        pieces = [mine[i]] + [a[i] + b[i] for a, b in zip(passed, came)]
        spec = sum([whole_lines(piece, lines, 2 * table.shape[1]) for piece in pieces], [])
        work_ref[i] = keep_valid(contract(table, jnp.concatenate(spec, axis=0), wide), lev, wave, modes)
    found = in_order(work_ref[...], order_ref[...])
    kept_ref[...], sent_ref[...] = found[:, :degrees], found[:, degrees:]


def finish_kernel(start, info_ref, waves_ref, *refs):
    out_ref, mark_ref = refs[-2:]
    mark_ref[...] = jnp.zeros_like(mark_ref)
    pairs = refs[0].shape[0]
    core = lax.rem(info_ref[0], 2)
    first = info_ref[0] < 2
    for side, (low, high, back) in enumerate((refs[:3], refs[3:6])):
        half = core if side == 0 else 1 - core
        for i in range(pairs):
            q = start + pl.program_id(0) * pairs + i
            swapped = waves_ref[half, 2 * q] > waves_ref[half, 2 * q + 1]
            out_ref[half, 2 * i + jnp.where(swapped, 1, 0)] = low[i]
            out_ref[half, 2 * i + jnp.where(swapped, 0, 1)] = jnp.where(first, back[i], high[i])


def block_pairs(start, pairs):
    for size in (8, 4, 2):
        if start % size == 0 and pairs % size == 0:
            return size
    return pairs if start % pairs == 0 else 1


def over_pairs(kernel, name, steps, info, waves, operands, in_specs, outs, out_specs, scratch=(), alias=None, after=()):
    operands = [*operands, *after]
    in_specs = [*in_specs, *[ANY] * len(after)]
    return pl.pallas_call(
        kernel,
        grid_spec=pltpu.PrefetchScalarGridSpec(
            num_scalar_prefetch=2,
            grid=(steps,),
            in_specs=in_specs,
            out_specs=(*out_specs, pl.BlockSpec((8, LANES), lambda *_: (0, 0))),
            scratch_shapes=list(scratch),
        ),
        out_shape=(*outs, MARK),
        input_output_aliases={} if alias is None else {2 + alias: 0},
        compiler_params=params(),
        cost_estimate=SMALL,
        name=name,
    )(info, waves, *operands)


def table_specs(start, block, table):
    slots, degrees, half = table.shape
    ahead = slots // 2 // (2 * block)
    offset = start // block
    place = lambda i, info, _: (lax.rem(info[0], 2) * ahead + offset + i, 0, 0)
    return [pl.BlockSpec((2 * block, degrees, half), place)] * 2


class Piece:
    def __init__(self, array, ahead=0, which=None):
        self.array, self.ahead, self.which = array, ahead, which

    def spec(self, block):
        shape = self.array.shape[-2:]
        offset, which = self.ahead // block, self.which
        last = self.array.shape[-3] // block - 1
        if which is None:
            return pl.BlockSpec((block, *shape), lambda i, *_: (jnp.clip(offset + i, 0, last), 0, 0))
        return pl.BlockSpec((None, block, *shape), lambda i, *_: (which, jnp.clip(offset + i, 0, last), 0, 0))


def give_kernel(start, info_ref, waves_ref, own_ref, other_ref, *refs):
    out_ref, mark_ref = refs[-2:]
    pairs, lines, _ = out_ref.shape
    mark_ref[...] = jnp.zeros_like(mark_ref)
    for i in range(pairs):
        swapped, _, _ = pair_of(waves_ref, start + pl.program_id(0) * pairs + i)
        table = chip_table(own_ref, other_ref, 2 * i + jnp.where(swapped, 0, 1))
        rows, half = table.shape
        if not packs(rows, half):
            out_ref[i] = table
            continue
        whole = half // LANES
        for b in range(whole):
            out_ref[i, b * rows : (b + 1) * rows] = table[:, b * LANES : (b + 1) * LANES]
        rest = table[:, whole * LANES :]
        out_ref[i, whole * rows :] = jnp.concatenate([rest[: rows // 2], rest[rows // 2 :]], axis=1)


def packs(rows, half):
    return half % LANES == LANES // 2 and rows % 32 == 0


def unpacked(block, rows, half):
    if not packs(rows, half):
        return block
    whole = half // LANES
    rest = block[whole * rows :]
    rest = jnp.concatenate([rest[:, : LANES // 2], rest[:, LANES // 2 :]], axis=0)
    return jnp.concatenate([block[b * rows : (b + 1) * rows] for b in range(whole)] + [rest], axis=1)


def gate_kernel(*refs):
    pass


def gate(arrays, after):
    count = len(arrays)
    found = pl.pallas_call(
        gate_kernel,
        in_specs=[ANY] * (count + len(after)),
        out_specs=(ANY,) * (count + 1),
        out_shape=(*[jax.ShapeDtypeStruct(a.shape, a.dtype) for a in arrays], MARK),
        input_output_aliases={i: i for i in range(count)},
        compiler_params=params(),
        cost_estimate=SMALL,
        name="gate",
    )(*arrays, *after)
    return found[:count], found[count]


def on_cores(chip_pairs):
    return [(2 * a + core, 2 * b + core) for a, b in chip_pairs for core in range(2)]


def send(block, pairs):
    return lax.ppermute(block, "lev", on_cores(pairs))


class Links:
    def __init__(self):
        self.mark = ()

    def send(self, block, pairs, after=(), meanwhile=()):
        after = tuple(mark for mark in after if mark is not None)
        if self.mark or after:
            (block,), _ = gate([block], (*self.mark, *after))
        (there,), mark = gate([send(block, pairs)], tuple(mark for mark in meanwhile if mark is not None))
        self.mark = (mark,)
        return block, there, mark


INWARD = [(0, 1), (3, 2)]
CENTRE = [(1, 2), (2, 1)]
OUTWARD = [(1, 0), (2, 3)]
GIVE = [(0, 1)]
RETURN = [(1, 0)]
SOURCES = [[0, 1, 2, 3], [1, 0, 2, 3], [2, 3, 1, 0], [3, 2, 1, 0]]


def chunk_sizes(pairs):
    if pairs % 40 == 0:
        return [pairs // 5, 2 * pairs // 5, 2 * pairs // 5]
    return [pairs]


def laid_out(sizes):
    found, start = [], 0
    for size in sizes:
        found.append((start, size))
        start += size
    return found


def given_parts(sizes):
    pairs = sum(sizes)
    if len(sizes) == 3 and pairs % 40 == 0:
        return laid_out([pairs // 5, pairs // 5, 3 * pairs // 10, 3 * pairs // 10])
    return laid_out([pairs] + [0] * len(sizes))


def per_device(grid_gradient, legendre, assign):
    fields, rows, nlon = grid_gradient.shape
    modes = nlon // 2
    slots, degrees, half = legendre.shape
    bands = lax.axis_size("lat")
    levels = lax.axis_size("lev")
    chips = levels // 2
    lat_id = lax.axis_index("lat")
    lev_id = lax.axis_index("lev")
    z, core = lev_id // 2, lev_id % 2
    groups = 2 * bands
    pairs = slots // 4
    wide = half // 256 * 256 if half >= 256 else half
    in_line = chips == 4
    sizes = chunk_sizes(pairs) if in_line else [pairs]
    chunks = laid_out(sizes)
    count = len(chunks)
    assign = assign.astype(jnp.int32)

    by_group = assign.reshape(groups, pairs, 2)
    listed = jnp.concatenate([by_group[:, s : s + n].reshape(groups * n, 2) for s, n in chunks])
    swapped = listed[:, 0] % 2 == 1
    even_wave = jnp.where(swapped, listed[:, 1], listed[:, 0])
    odd_wave = jnp.where(swapped, listed[:, 0], listed[:, 1])
    waves_of = jnp.stack([even_wave, odd_wave])
    first = (even_wave < odd_wave).astype(jnp.float32)[:, None]
    weight = jnp.where(waves_of == 0, 1.0, 2.0).astype(jnp.float32)[:, :, None]
    turn = 2.0 * math.pi / nlon

    def cos_sin(places, scale):
        angle = (waves_of[:, :, None] * places % nlon).astype(jnp.float32) * turn
        return jnp.stack([jnp.cos(angle) * scale, jnp.sin(angle) * scale], axis=1)

    base = cos_sin(jnp.arange(LANES, dtype=jnp.int32), weight)
    step = cos_sin(jnp.arange(0, modes, LANES, dtype=jnp.int32), 1.0)

    here = jnp.arange(rows, dtype=jnp.int32)
    wanted = jnp.where(lat_id >= bands // 2, rows - 1 - here, here)
    row_order = (here[None, :] == wanted[:, None]).astype(jnp.bfloat16)

    group_waves = lax.dynamic_slice(assign, (lat_id * slots,), (slots,)).reshape(2, slots // 2)
    waves = lax.dynamic_slice(group_waves, (core, 0), (1, slots // 2))[0]
    info = jnp.stack([lev_id])
    swap = [(i, i ^ 1) for i in range(levels)]
    squares = [[b * levels + 2 * chip + side for b in range(bands) for side in range(2)] for chip in range(chips)]
    other_table = lax.ppermute(legendre, "lev", swap)
    spec = {}
    state = {"mark": (), "out": None}

    def exchange(found):
        return lax.all_to_all(
            found, ("lat", "lev"), split_axis=0, concat_axis=0, axis_index_groups=squares, tiled=True
        )

    def zonal_first():
        found, *state["folded"], mark = fold_and_zonal(
            base, step, first, row_order, grid_gradient, groups, 0, sizes[:1], ()
        )
        state["mark"] = (mark,)
        spec[0] = (exchange(found), 0)

    def zonal_rest():
        found, mark = zonal(
            base, step, first, state["folded"], groups, groups * sizes[0], tuple(sizes[1:]), state["mark"]
        )
        state["mark"] = (mark,)
        arrived = exchange(found)
        for i in range(1, count):
            spec[i] = (arrived, chunks[i][0] - sizes[0])

    def do_halves(i):
        arrived, ahead = spec[i]
        both, again, low, mark = halves(arrived, fields, wide, ahead, sizes[i], state["mark"])
        state["mark"] = (mark,)
        return both, again, low, mark

    columns = chips * 4 * fields
    order_spec = pl.BlockSpec((columns, columns), lambda *_: (0, 0))

    lines = 4 * fields

    def high_slots(i, block, given, ends, pieces):
        s, n = chunks[i]
        shape = jax.ShapeDtypeStruct((n, degrees, columns), jnp.bfloat16)
        result = pl.BlockSpec((block, degrees, columns), lambda j, *_: (j, 0, 0))
        shape2 = jax.ShapeDtypeStruct((2, n, degrees, columns), jnp.bfloat16)
        result2 = pl.BlockSpec((2, block, degrees, columns), lambda j, *_: (0, j, 0, 0))
        parts = [*pieces, *given]
        return over_pairs(
            functools.partial(high_kernel, len(pieces), ends, lines, s, modes, wide), "high_slots", n // block, info,
            waves, [order, legendre, other_table, *[piece.array for piece in parts]],
            [order_spec, *table_specs(s, block, legendre), *[piece.spec(block) for piece in parts]],
            (shape2, shape, shape), (result2, result, result),
            [pltpu.VMEM((2 * block, 2 * degrees, columns), jnp.bfloat16)],
        )

    def low_slots(i, mine, passed, came):
        s, n = chunks[i]
        block = block_pairs(s, n)
        shape = jax.ShapeDtypeStruct((n, degrees, columns), jnp.bfloat16)
        result = pl.BlockSpec((block, degrees, columns), lambda j, *_: (j, 0, 0))
        parts = [mine, *passed, *came]
        return over_pairs(
            functools.partial(low_kernel, len(passed), lines, s, modes, wide), "low_slots", n // block, info, waves,
            [order, legendre, other_table, *[piece.array for piece in parts]],
            [order_spec, *table_specs(s, block, legendre), *[piece.spec(block) for piece in parts]],
            (shape, shape), (result, result),
            [pltpu.VMEM((block, 2 * degrees, columns), jnp.bfloat16)],
        )

    def finish(i, kept, got):
        s, n = chunks[i]
        block = block_pairs(s, n)
        before = () if state["out"] is None else (state["out"],)
        parts = [*kept, *got]
        state["out"], mark = over_pairs(
            functools.partial(finish_kernel, s), "finish", n // block, info, group_waves,
            [*[piece.array for piece in parts], *before],
            [*[piece.spec(block) for piece in parts], *[ANY] * len(before)],
            (jax.ShapeDtypeStruct((2, slots // 2, degrees, columns), jnp.bfloat16),),
            (pl.BlockSpec((2, 2 * block, degrees, columns), lambda j, *_: (0, s // block + j, 0, 0)),),
            alias=6 if before else None,
        )
        return mark

    if not in_line:
        zonal_first()
        both, _, _, _ = do_halves(0)
        sides = [[2 * chip + side for chip in range(chips)] for side in range(2)]
        everyone = lax.all_gather(both, "lev", axis=2, axis_index_groups=sides, tiled=True)
        order = column_order(jnp.arange(chips, dtype=jnp.int32), fields)
        given = Piece(jnp.zeros((pairs, 2 * degrees, half), jnp.bfloat16))
        high, sent, _, _ = high_slots(0, pairs, [given], [1], [Piece(everyone, 0, 1)])
        got_high = Piece(lax.ppermute(sent, "lev", swap))
        high = Piece(high, 0, 0)
        low, sent, _ = low_slots(0, Piece(everyone, 0, 0), [], [])
        got_low = Piece(lax.ppermute(sent, "lev", swap))
        finish(0, [Piece(low), high, high], [got_low, got_high, got_high])
        return state["out"].reshape(slots, degrees, columns)

    sources = jnp.array(SOURCES, jnp.int32)[z]
    order = column_order(sources, fields)
    parts = given_parts(sizes)
    gives = len(parts)
    ready, table, give_mark, table_mark = [[None] * gives for _ in range(4)]
    both, again, low, halves_mark = [[None] * count for _ in range(4)]
    high, got_high, high_mark, found_low, got_low, low_mark, back, returned = [[None] * count for _ in range(8)]
    first_in, first_cross, second_cross = [[None] * count for _ in range(3)]
    first_out, second_out, third_out = [[None] * count for _ in range(3)]
    in_mark, out_mark, out2_mark, out3_mark = [[None] * count for _ in range(4)]
    finish_mark = [None] * count
    inward, centre, outward = Links(), Links(), Links()
    last = count - 1

    def at(marks, i):
        return marks[i] if 0 <= i < len(marks) else None

    def do_give(i):
        s, n = parts[i] if i < gives else (0, 0)
        if n:
            block = block_pairs(s, n)
            line = (2 * degrees * half // LANES, LANES) if packs(2 * degrees, half) else (2 * degrees, half)
            ready[i], give_mark[i] = over_pairs(
                functools.partial(give_kernel, s), "give", n // block, info, waves, [legendre, other_table],
                table_specs(s, block, legendre), (jax.ShapeDtypeStruct((n, *line), jnp.bfloat16),),
                (pl.BlockSpec((block, *line), lambda j, *_: (j, 0, 0)),), after=state["mark"],
            )
            state["mark"] = (give_mark[i],)

    def send_table(i):
        if ready[i] is not None:
            _, table[i], table_mark[i] = inward.send(ready[i], GIVE)

    def prepare(i):
        both[i], again[i], low[i], halves_mark[i] = do_halves(i)

    def send_in(i):
        again[i], first_in[i], in_mark[i] = inward.send(again[i], INWARD)

    def send_cross(i):
        after = (at(out3_mark, i - 2),)
        meanwhile = (at(high_mark, i - 1), at(give_mark, i + 1), at(halves_mark, i + 1) if i else None)
        both[i], first_cross[i], _ = centre.send(both[i], CENTRE, after, meanwhile)

    def send_cross2(i):
        after = (at(out2_mark, i - 1),)
        meanwhile = (at(halves_mark, 1) if i == 0 else None, at(low_mark, i - 1))
        first_in[i], second_cross[i], _ = centre.send(first_in[i], CENTRE, after, meanwhile)

    def send_out():
        low[0], found, out_mark[0] = outward.send(low[0], OUTWARD, (), (halves_mark[1],))
        first_out[0] = Piece(found)

    def send_out2(i):
        meanwhile = ()
        blocks = [first_cross[i][0]]
        if i < last:
            blocks.append(low[i + 1])
        if i > 0:
            blocks.append(returned[i - 1])
        _, found, out2_mark[i] = outward.send(jnp.concatenate(blocks), OUTWARD, (), meanwhile)
        second_out[i] = Piece(found)
        ahead = sizes[i]
        if i < last:
            first_out[i + 1] = Piece(found, ahead)
            ahead += sizes[i + 1]
        if i > 0:
            came_back(i - 1, found, ahead)

    def came_back(i, found, ahead):
        found = found.reshape(2 * found.shape[0], degrees, columns)
        back[i] = [Piece(found, 2 * ahead), Piece(found, 2 * ahead + sizes[i])]

    def do_high(i):
        pieces = [Piece(passed[i], 0, 1) for passed in (both, first_in, first_cross, second_cross)]
        s, n = chunks[i]
        block = math.gcd(block_pairs(s, n), *[start for start, _ in parts if s < start < s + n])
        given, ends = [], []
        for (start, size), array in zip(parts, table):
            if max(s, start) < min(s + n, start + size):
                given.append(Piece(array, s - start))
                ends.append((start + size - s) // block)
        high[i], sent, sent_back, high_mark[i] = high_slots(i, block, given, ends, pieces)
        got_high[i] = lax.ppermute(sent, "lev", swap)
        got_back = lax.ppermute(sent_back, "lev", swap)
        returned[i] = jnp.concatenate([high[i][1], got_back]).reshape(second_cross[i].shape[1:])

    def send_out3(i):
        meanwhile = (at(table_mark, i + 1),) if i == last else ()
        _, found, out3_mark[i] = outward.send(second_cross[i][0], OUTWARD, (), meanwhile)
        third_out[i] = Piece(found)

    def send_back(i):
        _, found, _ = outward.send(returned[i], RETURN, (), (at(finish_mark, i - 1), at(low_mark, i)))
        came_back(i, found, 0)

    def do_low(i):
        passed = [Piece(array[i], 0, 0) for array in (first_in, first_cross, second_cross)]
        found_low[i], sent, low_mark[i] = low_slots(
            i, Piece(both[i], 0, 0), passed, [first_out[i], second_out[i], third_out[i]]
        )
        got_low[i] = lax.ppermute(sent, "lev", swap)

    def do_finish(i):
        finish_mark[i] = finish(
            i,
            [Piece(found_low[i]), Piece(high[i], 0, 0), back[i][0]],
            [Piece(got_low[i]), Piece(got_high[i]), back[i][1]],
        )

    zonal_first()
    do_give(0)
    send_table(0)
    if count > 1:
        zonal_rest()
    prepare(0)
    send_in(0)
    do_give(1)
    send_cross(0)
    prepare(1)
    send_out()
    for i in range(count):
        send_table(i + 1)
        if i < last:
            send_in(i + 1)
        send_out2(i)
        if i > 0:
            do_low(i - 1)
            do_finish(i - 1)
        send_cross2(i)
        do_high(i)
        do_give(i + 2)
        if i + 2 < count:
            prepare(i + 2)
        if i < last:
            send_cross(i + 1)
        send_out3(i)
    do_low(last)
    send_back(last)
    do_finish(last)
    return state["out"].reshape(slots, degrees, columns)


def solution(mesh):
    in_specs = (P("lev", "lat", None), P("lat", "lev", None), P())
    out_specs = P("lat", "lev", None)
    return jax.shard_map(
        per_device, mesh=mesh, in_specs=in_specs, out_specs=out_specs, check_vma=False
    )
```

```python
import functools
import math

import jax
import jax.numpy as jnp
from jax import lax
from jax.experimental import pallas as pl
from jax.experimental.pallas import tpu as pltpu
from jax.sharding import PartitionSpec as P

LANES = 128
VMEM_LIMIT = 48 * 1024 * 1024
MARK = jax.ShapeDtypeStruct((8, LANES), jnp.float32)
MARK_SPEC = pl.BlockSpec((8, LANES), lambda *_: (0, 0))
ANY = pl.BlockSpec(memory_space=pl.ANY)
SMALL = pl.CostEstimate(flops=1000, bytes_accessed=1000, transcendentals=0)


def dot_nt(a, b):
    return lax.dot_general(a, b, (((1,), (1,)), ((), ())), preferred_element_type=jnp.float32)


def params():
    return pltpu.CompilerParams(vmem_limit_bytes=VMEM_LIMIT)


def hi_lo(x):
    hi = x.astype(jnp.bfloat16)
    return hi, (x - hi.astype(jnp.float32)).astype(jnp.bfloat16)


def build_table(start, count, base_ref, step_ref, table_ref):
    for parity in range(2):
        cos0 = base_ref[parity, 0, start : start + count]
        sin0 = base_ref[parity, 1, start : start + count]
        for b in range(step_ref.shape[3]):
            cos1 = step_ref[parity, 0, start : start + count, b : b + 1]
            sin1 = step_ref[parity, 1, start : start + count, b : b + 1]
            both = (cos0 * cos1 - sin0 * sin1, -(sin0 * cos1 + cos0 * sin1))
            for c, table in enumerate(both):
                for part, term in enumerate(hi_lo(table)):
                    at = (2 * part + c) * count
                    table_ref[parity, at : at + count, b * LANES : (b + 1) * LANES] = term


def transform(start, sizes, first_ref, table_ref, folded, out_ref):
    groups = out_ref.shape[0]
    count = groups * sum(sizes)
    found = []
    for parity in range(2):
        main = dot_nt(table_ref[parity], folded[2 * parity])
        found.append(
            main[: 2 * count] + (main[2 * count :] + dot_nt(table_ref[parity, : 2 * count], folded[2 * parity + 1]))
        )
    first = first_ref[start : start + count] > 0.5
    chosen = []
    for left, right in (found, found[::-1]):
        for c in range(2):
            at = slice(c * count, (c + 1) * count)
            chosen.append(jnp.where(first, left[at], right[at]))
    for g in range(groups):
        rows, ahead = [], 0
        for pairs in sizes:
            rows += [values[ahead + g * pairs : ahead + (g + 1) * pairs] for values in chosen]
            ahead += groups * pairs
        out_ref[g] = jnp.concatenate(rows, axis=0).astype(jnp.bfloat16)


def fold_kernel(start, sizes, group, base_ref, step_ref, first_ref, order_ref, *refs):
    fields, refs = refs[:group], refs[-7:]
    out_ref, folded_refs, mark_ref, table_ref = refs[0], refs[1:5], refs[5], refs[6]
    mark_ref[...] = jnp.zeros_like(mark_ref)
    rows, half = order_ref.shape[0], folded_refs[0].shape[1]
    count = out_ref.shape[0] * sum(sizes)

    @pl.when(pl.program_id(0) == 0)
    def _():
        build_table(start, count, base_ref, step_ref, table_ref)

    for f, grid_ref in enumerate(fields):
        near, far = grid_ref[0, :, :half], grid_ref[0, :, half:]
        for parity, folded in enumerate((near + far, near - far)):
            for part, term in enumerate(hi_lo(folded)):
                moved = jnp.dot(order_ref[...], term, preferred_element_type=jnp.float32)
                folded_refs[2 * parity + part][f * rows : (f + 1) * rows] = moved.astype(jnp.bfloat16)
    transform(start, sizes, first_ref, table_ref, [ref[...] for ref in folded_refs], out_ref)


def fold_and_zonal(base, step, first, order, grid, groups, start, sizes, after):
    fields, rows, nlon = grid.shape
    half = nlon // 2
    group = 4 if fields % 4 == 0 and 4 * rows % LANES == 0 else fields
    pairs = sum(sizes)
    count = groups * pairs
    whole = [pl.BlockSpec(a.shape, lambda n, r=a.ndim: (0,) * r) for a in (base, step, first, order)]
    return pl.pallas_call(
        functools.partial(fold_kernel, start, sizes, group),
        grid=(fields // group,),
        in_specs=whole
        + [pl.BlockSpec((1, rows, nlon), lambda n, f=f: (n * group + f, 0, 0)) for f in range(group)]
        + [ANY] * len(after),
        out_specs=(
            pl.BlockSpec((groups, 4 * pairs, group * rows), lambda n: (0, 0, n)),
            *[pl.BlockSpec((group * rows, half), lambda n: (n, 0))] * 4,
            MARK_SPEC,
        ),
        out_shape=(
            jax.ShapeDtypeStruct((groups, 4 * pairs, fields * rows), jnp.bfloat16),
            *[jax.ShapeDtypeStruct((fields * rows, half), jnp.bfloat16)] * 4,
            MARK,
        ),
        scratch_shapes=[pltpu.VMEM((2, 4 * count, half), jnp.bfloat16)],
        compiler_params=params(),
        cost_estimate=SMALL,
        name="fold_and_zonal",
    )(base, step, first, order, *[grid] * group, *after)


def zonal_kernel(start, sizes, base_ref, step_ref, first_ref, *refs):
    folded, (out_ref, mark_ref, table_ref) = refs[:4], refs[-3:]
    count = out_ref.shape[0] * sum(sizes)
    mark_ref[...] = jnp.zeros_like(mark_ref)

    @pl.when(pl.program_id(0) == 0)
    def _():
        build_table(start, count, base_ref, step_ref, table_ref)

    transform(start, sizes, first_ref, table_ref, [ref[...] for ref in folded], out_ref)


def zonal(base, step, first, folded, groups, start, sizes, after):
    columns, half = folded[0].shape
    block = columns // 5 if columns % (5 * LANES) == 0 else columns
    pairs = sum(sizes)
    count = groups * pairs
    whole = [pl.BlockSpec(a.shape, lambda n, r=a.ndim: (0,) * r) for a in (base, step, first)]
    return pl.pallas_call(
        functools.partial(zonal_kernel, start, sizes),
        grid=(columns // block,),
        in_specs=whole + [pl.BlockSpec((block, half), lambda n: (n, 0))] * 4 + [ANY] * len(after),
        out_specs=(pl.BlockSpec((groups, 4 * pairs, block), lambda n: (0, 0, n)), MARK_SPEC),
        out_shape=(jax.ShapeDtypeStruct((groups, 4 * pairs, columns), jnp.bfloat16), MARK),
        scratch_shapes=[pltpu.VMEM((2, 4 * count, half), jnp.bfloat16)],
        compiler_params=params(),
        cost_estimate=SMALL,
        name="zonal",
    )(base, step, first, *folded, *after)


def halves_kernel(fields, wide, in_ref, *refs):
    both_ref, again_ref, low_ref, mark_ref, work_ref = refs[-5:]
    mark_ref[...] = jnp.zeros_like(mark_ref)
    bands = in_ref.shape[0] // 2
    pairs, lines, length = work_ref.shape
    rows = in_ref.shape[2] // fields
    for which in range(2):
        for core in range(2):
            for c in range(2):
                at = slice((2 * which + c) * pairs, (2 * which + c + 1) * pairs)
                parts = [in_ref[2 * b + core].astype(jnp.float32)[at] for b in range(bands)]
                sums = [parts[b] + parts[bands - 1 - b] for b in range(bands // 2)]
                gaps = [parts[b] - parts[bands - 1 - b] for b in range(bands // 2)]
                for f in range(fields):
                    at = slice(f * rows, (f + 1) * rows)
                    even = jnp.concatenate([x[:, at] for x in sums], axis=1)
                    odd = jnp.concatenate([x[:, at] for x in gaps], axis=1)
                    whole = [even[:, :wide], odd[:, :wide], even[:, wide:], odd[:, wide:]]
                    work_ref[:, (2 * core + c) * fields + f, :] = jnp.concatenate(whole, axis=1)
        for b in range(length // LANES):
            found = work_ref[:, :, b * LANES : (b + 1) * LANES].astype(jnp.bfloat16)
            at = slice(b * lines, (b + 1) * lines)
            both_ref[which, :, at] = found
            again_ref[which, :, at] = found
            if which == 0:
                low_ref[:, at] = found


def halves(arrived, fields, wide, ahead, pairs, after):
    groups, _, columns = arrived.shape
    lines, length = 4 * fields, groups * columns // (2 * fields)
    shape = (pairs, lines * length // LANES, LANES)
    shapes = [(2, *shape), (2, *shape), shape]
    return pl.pallas_call(
        functools.partial(halves_kernel, fields, wide),
        grid=(1,),
        out_shape=(*[jax.ShapeDtypeStruct(each, jnp.bfloat16) for each in shapes], MARK),
        in_specs=[pl.BlockSpec((groups, 4 * pairs, columns), lambda _: (0, ahead // pairs, 0))] + [ANY] * len(after),
        out_specs=(*[pl.BlockSpec(each, lambda _, r=len(each): (0,) * r) for each in shapes], MARK_SPEC),
        scratch_shapes=[pltpu.VMEM((pairs, lines, length), jnp.float32)],
        compiler_params=params(),
        cost_estimate=SMALL,
        name="halves",
    )(arrived, *after)


def whole_lines(block, lines, length):
    tiles = length // LANES
    found = []
    for start in range(0, block.shape[0], tiles * lines):
        found.append(
            jnp.concatenate([block[start + b * lines : start + (b + 1) * lines] for b in range(tiles)], axis=1)
        )
    return found


def contract(table, spec, wide):
    half = spec.shape[1] // 2
    count = spec.shape[0]
    even_row = lax.rem(lax.broadcasted_iota(jnp.int32, (table.shape[0], 1), 0), 2) == 0
    main = dot_nt(table[:, :wide], jnp.concatenate([spec[:, :wide], spec[:, wide : 2 * wide]], axis=0))
    total = jnp.where(even_row, main[:, :count], main[:, count:])
    if half > wide:
        rest = table[:, wide:].astype(jnp.float32)
        rest = jnp.concatenate([jnp.where(even_row, rest, 0.0), jnp.where(even_row, 0.0, rest)], axis=1)
        total = total + dot_nt(rest.astype(jnp.bfloat16), spec[:, 2 * wide :])
    return total


def keep_valid(values, lev, wave, modes):
    degrees = values.shape[0] // 2
    row = lax.broadcasted_iota(jnp.int32, (values.shape[0], 1), 0)
    other = lev + 1 - 2 * lax.rem(lev, 2)
    degree = jnp.where(row < degrees, lev * degrees + row, other * degrees + row - degrees)
    return jnp.where(degree < modes - wave, values, 0.0).astype(jnp.bfloat16)


def column_order(sources, fields):
    count = sources.shape[0] * 4 * fields
    row = jnp.arange(count, dtype=jnp.int32)
    chip = jnp.repeat(sources, 4 * fields)
    core = row // (2 * fields) % 2
    c = row // fields % 2
    target = c * (count // 2) + (2 * chip + core) * fields + row % fields
    return (row[None, :] == target[:, None]).astype(jnp.bfloat16)


def in_order(values, order):
    count, degrees, columns = values.shape
    moved = jnp.dot(values.reshape(count * degrees, columns), order, preferred_element_type=jnp.float32)
    return moved.astype(jnp.bfloat16).reshape(count, degrees, columns)


def chip_table(own_ref, other_ref, slot):
    return jnp.concatenate([own_ref[slot], other_ref[slot]], axis=0)


def pair_of(waves_ref, q):
    left, right = waves_ref[2 * q], waves_ref[2 * q + 1]
    return left > right, jnp.minimum(left, right), jnp.maximum(left, right)


def high_kernel(parts, ends, lines, start, modes, wide, info_ref, waves_ref, order_ref, own_ref, other_ref, *refs):
    pieces, (kept_ref, sent_ref, sent_back_ref, mark_ref, work_ref) = refs[:parts], refs[-5:]
    given = refs[parts : parts + len(ends)]
    mark_ref[...] = jnp.zeros_like(mark_ref)
    _, pairs, degrees, _ = kept_ref.shape
    lev = info_ref[0]
    for i in range(pairs):
        swapped, _, wave = pair_of(waves_ref, start + pl.program_id(0) * pairs + i)
        table = chip_table(own_ref, other_ref, 2 * i + jnp.where(swapped, 0, 1))
        block = given[-1][i]
        for ref, end in zip(given[-2::-1], ends[-2::-1]):
            block = jnp.where(pl.program_id(0) < end, ref[i], block)
        both = jnp.concatenate([table, unpacked(block, *table.shape)], axis=0)
        spec = sum([whole_lines(piece[i], lines, 2 * table.shape[1]) for piece in pieces], [])
        values = contract(both, jnp.concatenate(spec, axis=0), wide)
        work_ref[i] = keep_valid(values[: 2 * degrees], lev, wave, modes)
        work_ref[pairs + i] = keep_valid(values[2 * degrees :], lev - 2, wave, modes)
    for which in range(2):
        found = in_order(work_ref[which * pairs : (which + 1) * pairs], order_ref[...])
        kept_ref[which] = found[:, :degrees]
        (sent_ref, sent_back_ref)[which][...] = found[:, degrees:]


def low_kernel(parts, lines, start, modes, wide, info_ref, waves_ref, order_ref, own_ref, other_ref, *refs):
    mine, passed, came = refs[0], refs[1 : 1 + parts], refs[1 + parts : 1 + 2 * parts]
    kept_ref, sent_ref, mark_ref, work_ref = refs[-4:]
    mark_ref[...] = jnp.zeros_like(mark_ref)
    pairs, degrees, _ = kept_ref.shape
    lev = info_ref[0]
    for i in range(pairs):
        swapped, wave, _ = pair_of(waves_ref, start + pl.program_id(0) * pairs + i)
        table = chip_table(own_ref, other_ref, 2 * i + jnp.where(swapped, 1, 0))
        pieces = [mine[i]] + [a[i] + b[i] for a, b in zip(passed, came)]
        spec = sum([whole_lines(piece, lines, 2 * table.shape[1]) for piece in pieces], [])
        work_ref[i] = keep_valid(contract(table, jnp.concatenate(spec, axis=0), wide), lev, wave, modes)
    found = in_order(work_ref[...], order_ref[...])
    kept_ref[...], sent_ref[...] = found[:, :degrees], found[:, degrees:]


def finish_kernel(start, info_ref, waves_ref, *refs):
    out_ref, mark_ref = refs[-2:]
    mark_ref[...] = jnp.zeros_like(mark_ref)
    pairs = refs[0].shape[0]
    core = lax.rem(info_ref[0], 2)
    first = info_ref[0] < 2
    for side, (low, high, back) in enumerate((refs[:3], refs[3:6])):
        half = core if side == 0 else 1 - core
        for i in range(pairs):
            q = start + pl.program_id(0) * pairs + i
            swapped = waves_ref[half, 2 * q] > waves_ref[half, 2 * q + 1]
            out_ref[half, 2 * i + jnp.where(swapped, 1, 0)] = low[i]
            out_ref[half, 2 * i + jnp.where(swapped, 0, 1)] = jnp.where(first, back[i], high[i])


def block_pairs(start, pairs):
    for size in (8, 4, 2):
        if start % size == 0 and pairs % size == 0:
            return size
    return pairs if start % pairs == 0 else 1


def over_pairs(kernel, name, steps, info, waves, operands, in_specs, outs, out_specs, scratch=(), alias=None, after=()):
    operands = [*operands, *after]
    in_specs = [*in_specs, *[ANY] * len(after)]
    return pl.pallas_call(
        kernel,
        grid_spec=pltpu.PrefetchScalarGridSpec(
            num_scalar_prefetch=2,
            grid=(steps,),
            in_specs=in_specs,
            out_specs=(*out_specs, pl.BlockSpec((8, LANES), lambda *_: (0, 0))),
            scratch_shapes=list(scratch),
        ),
        out_shape=(*outs, MARK),
        input_output_aliases={} if alias is None else {2 + alias: 0},
        compiler_params=params(),
        cost_estimate=SMALL,
        name=name,
    )(info, waves, *operands)


def table_specs(start, block, table):
    slots, degrees, half = table.shape
    ahead = slots // 2 // (2 * block)
    offset = start // block
    place = lambda i, info, _: (lax.rem(info[0], 2) * ahead + offset + i, 0, 0)
    return [pl.BlockSpec((2 * block, degrees, half), place)] * 2


class Piece:
    def __init__(self, array, ahead=0, which=None):
        self.array, self.ahead, self.which = array, ahead, which

    def spec(self, block):
        shape = self.array.shape[-2:]
        offset, which = self.ahead // block, self.which
        last = self.array.shape[-3] // block - 1
        if which is None:
            return pl.BlockSpec((block, *shape), lambda i, *_: (jnp.clip(offset + i, 0, last), 0, 0))
        return pl.BlockSpec((None, block, *shape), lambda i, *_: (which, jnp.clip(offset + i, 0, last), 0, 0))


def give_kernel(start, info_ref, waves_ref, own_ref, other_ref, *refs):
    out_ref, mark_ref = refs[-2:]
    pairs, lines, _ = out_ref.shape
    mark_ref[...] = jnp.zeros_like(mark_ref)
    for i in range(pairs):
        swapped, _, _ = pair_of(waves_ref, start + pl.program_id(0) * pairs + i)
        table = chip_table(own_ref, other_ref, 2 * i + jnp.where(swapped, 0, 1))
        rows, half = table.shape
        if not packs(rows, half):
            out_ref[i] = table
            continue
        whole = half // LANES
        for b in range(whole):
            out_ref[i, b * rows : (b + 1) * rows] = table[:, b * LANES : (b + 1) * LANES]
        rest = table[:, whole * LANES :]
        out_ref[i, whole * rows :] = jnp.concatenate([rest[: rows // 2], rest[rows // 2 :]], axis=1)


def packs(rows, half):
    return half % LANES == LANES // 2 and rows % 32 == 0


def unpacked(block, rows, half):
    if not packs(rows, half):
        return block
    whole = half // LANES
    rest = block[whole * rows :]
    rest = jnp.concatenate([rest[:, : LANES // 2], rest[:, LANES // 2 :]], axis=0)
    return jnp.concatenate([block[b * rows : (b + 1) * rows] for b in range(whole)] + [rest], axis=1)


def gate_kernel(*refs):
    pass


def gate(arrays, after):
    count = len(arrays)
    found = pl.pallas_call(
        gate_kernel,
        in_specs=[ANY] * (count + len(after)),
        out_specs=(ANY,) * (count + 1),
        out_shape=(*[jax.ShapeDtypeStruct(a.shape, a.dtype) for a in arrays], MARK),
        input_output_aliases={i: i for i in range(count)},
        compiler_params=params(),
        cost_estimate=SMALL,
        name="gate",
    )(*arrays, *after)
    return found[:count], found[count]


def on_cores(chip_pairs):
    return [(2 * a + core, 2 * b + core) for a, b in chip_pairs for core in range(2)]


def send(block, pairs):
    return lax.ppermute(block, "lev", on_cores(pairs))


class Links:
    def __init__(self):
        self.mark = ()

    def send(self, block, pairs, after=(), meanwhile=()):
        after = tuple(mark for mark in after if mark is not None)
        if self.mark or after:
            (block,), _ = gate([block], (*self.mark, *after))
        (there,), mark = gate([send(block, pairs)], tuple(mark for mark in meanwhile if mark is not None))
        self.mark = (mark,)
        return block, there, mark


INWARD = [(0, 1), (3, 2)]
CENTRE = [(1, 2), (2, 1)]
OUTWARD = [(1, 0), (2, 3)]
GIVE = [(0, 1)]
RETURN = [(1, 0)]
SOURCES = [[0, 1, 2, 3], [1, 0, 2, 3], [2, 3, 1, 0], [3, 2, 1, 0]]


def chunk_sizes(pairs):
    if pairs % 40 == 0:
        return [pairs // 5, 2 * pairs // 5, 2 * pairs // 5]
    return [pairs]


def laid_out(sizes):
    found, start = [], 0
    for size in sizes:
        found.append((start, size))
        start += size
    return found


def given_parts(sizes):
    pairs = sum(sizes)
    if len(sizes) == 3 and pairs % 40 == 0:
        return laid_out([pairs // 5, pairs // 5, 3 * pairs // 10, 3 * pairs // 10])
    return laid_out([pairs] + [0] * len(sizes))


def per_device(grid_gradient, legendre, assign):
    fields, rows, nlon = grid_gradient.shape
    modes = nlon // 2
    slots, degrees, half = legendre.shape
    bands = lax.axis_size("lat")
    levels = lax.axis_size("lev")
    chips = levels // 2
    lat_id = lax.axis_index("lat")
    lev_id = lax.axis_index("lev")
    z, core = lev_id // 2, lev_id % 2
    groups = 2 * bands
    pairs = slots // 4
    wide = half // 256 * 256 if half >= 256 else half
    in_line = chips == 4
    sizes = chunk_sizes(pairs) if in_line else [pairs]
    chunks = laid_out(sizes)
    count = len(chunks)
    assign = assign.astype(jnp.int32)

    by_group = assign.reshape(groups, pairs, 2)
    listed = jnp.concatenate([by_group[:, s : s + n].reshape(groups * n, 2) for s, n in chunks])
    swapped = listed[:, 0] % 2 == 1
    even_wave = jnp.where(swapped, listed[:, 1], listed[:, 0])
    odd_wave = jnp.where(swapped, listed[:, 0], listed[:, 1])
    waves_of = jnp.stack([even_wave, odd_wave])
    first = (even_wave < odd_wave).astype(jnp.float32)[:, None]
    weight = jnp.where(waves_of == 0, 1.0, 2.0).astype(jnp.float32)[:, :, None]
    turn = 2.0 * math.pi / nlon

    def cos_sin(places, scale):
        angle = (waves_of[:, :, None] * places % nlon).astype(jnp.float32) * turn
        return jnp.stack([jnp.cos(angle) * scale, jnp.sin(angle) * scale], axis=1)

    base = cos_sin(jnp.arange(LANES, dtype=jnp.int32), weight)
    step = cos_sin(jnp.arange(0, modes, LANES, dtype=jnp.int32), 1.0)

    here = jnp.arange(rows, dtype=jnp.int32)
    wanted = jnp.where(lat_id >= bands // 2, rows - 1 - here, here)
    row_order = (here[None, :] == wanted[:, None]).astype(jnp.bfloat16)

    group_waves = lax.dynamic_slice(assign, (lat_id * slots,), (slots,)).reshape(2, slots // 2)
    waves = lax.dynamic_slice(group_waves, (core, 0), (1, slots // 2))[0]
    info = jnp.stack([lev_id])
    swap = [(i, i ^ 1) for i in range(levels)]
    squares = [[b * levels + 2 * chip + side for b in range(bands) for side in range(2)] for chip in range(chips)]
    other_table = lax.ppermute(legendre, "lev", swap)
    spec = {}
    state = {"mark": (), "out": None}

    def exchange(found):
        return lax.all_to_all(
            found, ("lat", "lev"), split_axis=0, concat_axis=0, axis_index_groups=squares, tiled=True
        )

    def zonal_first():
        found, *state["folded"], mark = fold_and_zonal(
            base, step, first, row_order, grid_gradient, groups, 0, sizes[:1], ()
        )
        state["mark"] = (mark,)
        spec[0] = (exchange(found), 0)

    def zonal_rest():
        found, mark = zonal(
            base, step, first, state["folded"], groups, groups * sizes[0], tuple(sizes[1:]), state["mark"]
        )
        state["mark"] = (mark,)
        arrived = exchange(found)
        for i in range(1, count):
            spec[i] = (arrived, chunks[i][0] - sizes[0])

    def do_halves(i):
        arrived, ahead = spec[i]
        both, again, low, mark = halves(arrived, fields, wide, ahead, sizes[i], state["mark"])
        state["mark"] = (mark,)
        return both, again, low, mark

    columns = chips * 4 * fields
    order_spec = pl.BlockSpec((columns, columns), lambda *_: (0, 0))

    lines = 4 * fields

    def high_slots(i, block, given, ends, pieces):
        s, n = chunks[i]
        shape = jax.ShapeDtypeStruct((n, degrees, columns), jnp.bfloat16)
        result = pl.BlockSpec((block, degrees, columns), lambda j, *_: (j, 0, 0))
        shape2 = jax.ShapeDtypeStruct((2, n, degrees, columns), jnp.bfloat16)
        result2 = pl.BlockSpec((2, block, degrees, columns), lambda j, *_: (0, j, 0, 0))
        parts = [*pieces, *given]
        return over_pairs(
            functools.partial(high_kernel, len(pieces), ends, lines, s, modes, wide), "high_slots", n // block, info,
            waves, [order, legendre, other_table, *[piece.array for piece in parts]],
            [order_spec, *table_specs(s, block, legendre), *[piece.spec(block) for piece in parts]],
            (shape2, shape, shape), (result2, result, result),
            [pltpu.VMEM((2 * block, 2 * degrees, columns), jnp.bfloat16)],
        )

    def low_slots(i, mine, passed, came):
        s, n = chunks[i]
        block = block_pairs(s, n)
        shape = jax.ShapeDtypeStruct((n, degrees, columns), jnp.bfloat16)
        result = pl.BlockSpec((block, degrees, columns), lambda j, *_: (j, 0, 0))
        parts = [mine, *passed, *came]
        return over_pairs(
            functools.partial(low_kernel, len(passed), lines, s, modes, wide), "low_slots", n // block, info, waves,
            [order, legendre, other_table, *[piece.array for piece in parts]],
            [order_spec, *table_specs(s, block, legendre), *[piece.spec(block) for piece in parts]],
            (shape, shape), (result, result),
            [pltpu.VMEM((block, 2 * degrees, columns), jnp.bfloat16)],
        )

    def finish(i, kept, got):
        s, n = chunks[i]
        block = block_pairs(s, n)
        before = () if state["out"] is None else (state["out"],)
        parts = [*kept, *got]
        state["out"], mark = over_pairs(
            functools.partial(finish_kernel, s), "finish", n // block, info, group_waves,
            [*[piece.array for piece in parts], *before],
            [*[piece.spec(block) for piece in parts], *[ANY] * len(before)],
            (jax.ShapeDtypeStruct((2, slots // 2, degrees, columns), jnp.bfloat16),),
            (pl.BlockSpec((2, 2 * block, degrees, columns), lambda j, *_: (0, s // block + j, 0, 0)),),
            alias=6 if before else None,
        )
        return mark

    if not in_line:
        zonal_first()
        both, _, _, _ = do_halves(0)
        sides = [[2 * chip + side for chip in range(chips)] for side in range(2)]
        everyone = lax.all_gather(both, "lev", axis=2, axis_index_groups=sides, tiled=True)
        order = column_order(jnp.arange(chips, dtype=jnp.int32), fields)
        given = Piece(jnp.zeros((pairs, 2 * degrees, half), jnp.bfloat16))
        high, sent, _, _ = high_slots(0, pairs, [given], [1], [Piece(everyone, 0, 1)])
        got_high = Piece(lax.ppermute(sent, "lev", swap))
        high = Piece(high, 0, 0)
        low, sent, _ = low_slots(0, Piece(everyone, 0, 0), [], [])
        got_low = Piece(lax.ppermute(sent, "lev", swap))
        finish(0, [Piece(low), high, high], [got_low, got_high, got_high])
        return state["out"].reshape(slots, degrees, columns)

    sources = jnp.array(SOURCES, jnp.int32)[z]
    order = column_order(sources, fields)
    parts = given_parts(sizes)
    gives = len(parts)
    ready, table, give_mark, table_mark = [[None] * gives for _ in range(4)]
    both, again, low, halves_mark = [[None] * count for _ in range(4)]
    high, got_high, high_mark, found_low, got_low, low_mark, back, returned = [[None] * count for _ in range(8)]
    first_in, first_cross, second_cross = [[None] * count for _ in range(3)]
    first_out, second_out, third_out = [[None] * count for _ in range(3)]
    in_mark, out_mark, out2_mark, out3_mark = [[None] * count for _ in range(4)]
    inward, centre, outward = Links(), Links(), Links()
    last = count - 1

    def at(marks, i):
        return marks[i] if 0 <= i < len(marks) else None

    def do_give(i):
        s, n = parts[i] if i < gives else (0, 0)
        if n:
            block = block_pairs(s, n)
            line = (2 * degrees * half // LANES, LANES) if packs(2 * degrees, half) else (2 * degrees, half)
            ready[i], give_mark[i] = over_pairs(
                functools.partial(give_kernel, s), "give", n // block, info, waves, [legendre, other_table],
                table_specs(s, block, legendre), (jax.ShapeDtypeStruct((n, *line), jnp.bfloat16),),
                (pl.BlockSpec((block, *line), lambda j, *_: (j, 0, 0)),), after=state["mark"],
            )
            state["mark"] = (give_mark[i],)

    def send_table(i):
        if ready[i] is not None:
            _, table[i], table_mark[i] = inward.send(ready[i], GIVE)

    def prepare(i):
        both[i], again[i], low[i], halves_mark[i] = do_halves(i)

    def send_in(i):
        again[i], first_in[i], in_mark[i] = inward.send(again[i], INWARD)

    def send_cross(i):
        after = (at(out3_mark, i - 2),)
        meanwhile = (at(high_mark, i - 1), at(give_mark, i + 1), at(halves_mark, i + 1) if i else None)
        both[i], first_cross[i], _ = centre.send(both[i], CENTRE, after, meanwhile)

    def send_cross2(i):
        after = ()
        meanwhile = (at(halves_mark, 1) if i == 0 else None, at(low_mark, i - 1))
        first_in[i], second_cross[i], _ = centre.send(first_in[i], CENTRE, after, meanwhile)

    def send_out():
        low[0], found, out_mark[0] = outward.send(low[0], OUTWARD, (), (halves_mark[1],))
        first_out[0] = Piece(found)

    def send_out2(i):
        meanwhile = ()
        blocks = [first_cross[i][0]]
        if i < last:
            blocks.append(low[i + 1])
        if i > 0:
            blocks.append(returned[i - 1])
        _, found, out2_mark[i] = outward.send(jnp.concatenate(blocks), OUTWARD, (), meanwhile)
        second_out[i] = Piece(found)
        ahead = sizes[i]
        if i < last:
            first_out[i + 1] = Piece(found, ahead)
            ahead += sizes[i + 1]
        if i > 0:
            came_back(i - 1, found, ahead)

    def came_back(i, found, ahead):
        found = found.reshape(2 * found.shape[0], degrees, columns)
        back[i] = [Piece(found, 2 * ahead), Piece(found, 2 * ahead + sizes[i])]

    def do_high(i):
        pieces = [Piece(passed[i], 0, 1) for passed in (both, first_in, first_cross, second_cross)]
        s, n = chunks[i]
        block = math.gcd(block_pairs(s, n), *[start for start, _ in parts if s < start < s + n])
        given, ends = [], []
        for (start, size), array in zip(parts, table):
            if max(s, start) < min(s + n, start + size):
                given.append(Piece(array, s - start))
                ends.append((start + size - s) // block)
        high[i], sent, sent_back, high_mark[i] = high_slots(i, block, given, ends, pieces)
        got_high[i] = lax.ppermute(sent, "lev", swap)
        got_back = lax.ppermute(sent_back, "lev", swap)
        returned[i] = jnp.concatenate([high[i][1], got_back]).reshape(second_cross[i].shape[1:])

    def send_out3(i):
        meanwhile = (at(table_mark, i + 1),) if i == last else ()
        _, found, out3_mark[i] = outward.send(second_cross[i][0], OUTWARD, (), meanwhile)
        third_out[i] = Piece(found)

    def send_back(i):
        _, found, _ = outward.send(returned[i], RETURN)
        came_back(i, found, 0)

    def do_low(i):
        passed = [Piece(array[i], 0, 0) for array in (first_in, first_cross, second_cross)]
        found_low[i], sent, low_mark[i] = low_slots(
            i, Piece(both[i], 0, 0), passed, [first_out[i], second_out[i], third_out[i]]
        )
        got_low[i] = lax.ppermute(sent, "lev", swap)

    def do_finish(i):
        finish(
            i,
            [Piece(found_low[i]), Piece(high[i], 0, 0), back[i][0]],
            [Piece(got_low[i]), Piece(got_high[i]), back[i][1]],
        )

    zonal_first()
    do_give(0)
    send_table(0)
    if count > 1:
        zonal_rest()
    prepare(0)
    send_in(0)
    do_give(1)
    send_cross(0)
    prepare(1)
    send_out()
    for i in range(count):
        send_table(i + 1)
        if i < last:
            send_in(i + 1)
        send_out2(i)
        if i > 0:
            do_low(i - 1)
            do_finish(i - 1)
        send_cross2(i)
        do_high(i)
        do_give(i + 2)
        if i + 2 < count:
            prepare(i + 2)
        if i < last:
            send_cross(i + 1)
        send_out3(i)
    send_back(last)
    do_low(last)
    do_finish(last)
    return state["out"].reshape(slots, degrees, columns)


def solution(mesh):
    in_specs = (P("lev", "lat", None), P("lat", "lev", None), P())
    out_specs = P("lat", "lev", None)
    return jax.shard_map(
        per_device, mesh=mesh, in_specs=in_specs, out_specs=out_specs, check_vma=False
    )
```
